512 devices in a mesh: seg: 32 (over y, z_lo, core), fsdp: 16 (over z_hi, x).
Axes of the slice: x: 4, y: 8, z: 8 (z_hi: 4, z_lo: 2; z = z_hi * 2 + z_lo), core: 2. Of those that a mesh axis runs over, the one named last changes fastest.
Arguments:
- tokens: bfloat16 [8192, 8192], P('seg'), may hold values from -72 to 72
- w_query: bfloat16 [8192, 4096], P('seg', 'fsdp'), may hold values from -0.0625 to 0.0625
- key_weight: bfloat16 [8192, 512], P('seg', 'fsdp'), may hold values from -0.0625 to 0.0625
- value_weight: bfloat16 [8192, 512], P('seg', 'fsdp'), may hold values from -0.0625 to 0.0625
- resid_head: bfloat16 [8192], replicated, may hold values from -0.0625 to 0.0625
- head_readout: bfloat16 [4096], P('fsdp'), may hold values from -1.5 to 1.5
- parents: int32 [32], replicated, may hold values from -1 to 29, as said below
- placed: int32 [32], replicated, may hold values from 0 to 31, each once
- lengths: int32 [32], replicated, may hold values from 32 to 256, as said below
Outputs:
- token_values: float32 [8192], P('seg')
- branch_values: float32 [32], replicated
The draws below stay inside these ranges and needn't reach their ends.
Inputs may be any that keep to these rules, and one draw needn't show every extreme that they name: parents[0] = -1 and parents[i] = i - 1 for 0 < i < 2; every other segment's parent has a smaller index, 1 or more. `placed`: a permutation. `lengths`: segments 0 to 1 are full.
All inputs are finite; a program needn't handle non-finite values.
Results may differ from the reference program's by a relative error of at most 0.015.
The reference program's roundings to bfloat16 on the way (of `query`, `key_proj`, `value_proj`, `weights` and `mixed`) count: a program that leaves them out, or rounds other values in their place, can miss the bound.
Values may be sent and summed in bfloat16 or wider, within the bound.
No kernel may reach another device: no remote copies, remote signals or barrier semaphores. Data moves between devices by JAX's collectives and lax.ppermute only.
A program may use at most 128 MiB of HBM per device.

```python
import jax
import jax.numpy as jnp
from jax import lax

MODEL_WIDTH = 8192
QUERY_HEADS = 32
KEY_VALUE_HEADS = 4
HEAD_SIZE = 128
SEG_LEN = 256
PROMPT_SEGS = 2
SEGS = 32
TOKENS = 8192


def draw_tokens(key, part):
    key = jax.random.fold_in(key, 1)
    first_key = jax.random.fold_in(key, 0)
    noise = jnp.clip(jax.random.normal(first_key, (TOKENS, MODEL_WIDTH), jnp.float32), -6.0, 6.0)
    return noise.astype(jnp.bfloat16)


def draw_parents(key, part):
    key = jax.random.fold_in(key, 2)
    bits_key, flip_key = jax.random.split(key)
    indices = jnp.arange(SEGS, dtype=jnp.int32)
    random_bits = jax.random.randint(bits_key, (SEGS,), 0, 1073741824, dtype=jnp.int32)
    lowest = PROMPT_SEGS - 1
    spread_count = jnp.maximum(indices - lowest, 1)
    chosen = lowest + random_bits % spread_count
    parent_ids = jnp.where(indices < PROMPT_SEGS, indices - 1, chosen)
    forced_index = SEGS - 2 + jax.random.randint(flip_key, (), 0, 2, dtype=jnp.int32)
    parent_ids = jnp.where(indices == forced_index, SEGS - 3, parent_ids)
    return parent_ids.astype(jnp.int32)


def draw_lengths(key, part):
    key = jax.random.fold_in(key, 3)
    indices = jnp.arange(SEGS, dtype=jnp.int32)
    drawn = jax.random.randint(key, (SEGS,), SEG_LEN // 8, SEG_LEN + 1, dtype=jnp.int32)
    return jnp.where(indices < PROMPT_SEGS, SEG_LEN, drawn).astype(jnp.int32)


def block_scale(key, extent, cuts, low, high):
    gain = 1.0
    for position, parts in cuts:
        heights = jax.random.uniform(jax.random.fold_in(jax.random.fold_in(key, 6), position), (parts,), jnp.float32, low / len(cuts), high / len(cuts))
        gain = gain * jnp.repeat(jnp.exp(heights), extent[position] // parts).reshape((-1,) + (1,) * (len(extent) - 1 - position))
    return gain


def centred(own_key, shape, spread, most, shards=(), held_as=jnp.bfloat16):
    array = jax.random.normal(own_key, shape, jnp.float32) * spread
    if len(shards) > 0:
        array = block_scale(own_key, shape, shards, -0.22, 0.18) * array
    return jnp.clip(array, min=-most, max=most).astype(held_as)


def setup_inputs(seed: int = 0) -> dict:
    key_of = jax.random.split(jax.random.key(seed), 10)
    tokens = draw_tokens(jax.random.fold_in(key_of[9], 71), 0)
    w_query = centred(key_of[1], (MODEL_WIDTH, QUERY_HEADS * HEAD_SIZE), MODEL_WIDTH ** -0.5, 0.0625, ((0, 32), (1, 16)))
    key_weight = centred(key_of[2], (MODEL_WIDTH, KEY_VALUE_HEADS * HEAD_SIZE), MODEL_WIDTH ** -0.5, 0.0625, ((0, 32), (1, 16)))
    value_weight = centred(key_of[3], (MODEL_WIDTH, KEY_VALUE_HEADS * HEAD_SIZE), MODEL_WIDTH ** -0.5, 0.0625, ((0, 32), (1, 16)))
    resid_head = centred(key_of[4], (MODEL_WIDTH,), MODEL_WIDTH ** -0.5, 0.0625)
    head_readout = centred(key_of[5], (QUERY_HEADS * HEAD_SIZE,), 0.25, 1.5, ((0, 16),))
    parents = draw_parents(jax.random.fold_in(key_of[9], 71), 0)
    placed = jax.random.permutation(key_of[7], SEGS).astype(jnp.int32)
    lengths = draw_lengths(jax.random.fold_in(key_of[9], 71), 0)
    return {"tokens": tokens, "w_query": w_query, "key_weight": key_weight, "value_weight": value_weight, "resid_head": resid_head, "head_readout": head_readout, "parents": parents, "placed": placed, "lengths": lengths}


rope_base = 1000000.0


def tree_tables(parents, lengths, placed):
    segments = parents.shape[0]
    identity = jnp.eye(segments, dtype=jnp.float32)

    def stepper(ancestors, segment):
        parent_id = parents[segment]
        above_row = lax.dynamic_index_in_dim(ancestors, jnp.maximum(parent_id, 0).astype(jnp.int32), 0, keepdims=False)
        row_value = jnp.where(parent_id >= 0, above_row, jnp.zeros_like(above_row)) + identity[segment]
        return lax.dynamic_update_index_in_dim(ancestors, row_value, segment, 0), None

    ancestry, _ = lax.scan(stepper, jnp.zeros((segments, segments), jnp.float32), jnp.arange(segments, dtype=jnp.int32))
    strict = ancestry - identity
    seg_ids = jnp.arange(segments, dtype=jnp.int32)
    lengths_real = lengths.astype(jnp.float32)
    offsets = jnp.dot(strict, lengths_real, precision=lax.Precision.HIGHEST)
    children = jnp.sum((parents[:, None] == seg_ids[None, :]).astype(jnp.float32), axis=0)
    leafy = (children < 0.5).astype(jnp.float32)
    placement = (placed[:, None] == seg_ids[None, :]).astype(jnp.float32)
    strict_slot = jnp.dot(jnp.dot(placement, strict, precision=lax.Precision.HIGHEST), placement.T, precision=lax.Precision.HIGHEST)
    length_slot = jnp.dot(placement, lengths_real, precision=lax.Precision.HIGHEST)
    offset_slot = jnp.dot(placement, offsets, precision=lax.Precision.HIGHEST)
    leaf_slot = jnp.dot(placement, leafy, precision=lax.Precision.HIGHEST)
    return ancestry, leafy, placement, strict_slot, length_slot, offset_slot, leaf_slot


def rope(projected, positions, pair_index):
    paired = projected.reshape(projected.shape[0], projected.shape[1] // 2, 2)
    frequency = rope_base ** (-2.0 * pair_index / HEAD_SIZE)
    angles = positions[:, None] * frequency[None, :]
    cosine = jnp.cos(angles)
    sine_part = jnp.sin(angles)
    first_part = paired[:, :, 0]
    second_part = paired[:, :, 1]
    turned = jnp.stack([first_part * cosine - second_part * sine_part, first_part * sine_part + second_part * cosine], axis=2)
    return turned.reshape(projected.shape)


def reference(tokens, w_query, key_weight, value_weight, resid_head, head_readout, parents, placed, lengths):
    ancestry, leafy, placement, strict_slot, length_slot, offset_slot, leaf_slot = tree_tables(parents, lengths, placed)
    token_ids = jnp.arange(TOKENS, dtype=jnp.int32)
    slot_of = token_ids // SEG_LEN
    index_of = token_ids % SEG_LEN
    index_real = index_of.astype(jnp.float32)
    positions = offset_slot[slot_of] + index_real
    pair_query = ((2 * jnp.arange(QUERY_HEADS * HEAD_SIZE // 2, dtype=jnp.int32)) % HEAD_SIZE // 2).astype(jnp.float32)
    partner_key = ((2 * jnp.arange(KEY_VALUE_HEADS * HEAD_SIZE // 2, dtype=jnp.int32)) % HEAD_SIZE // 2).astype(jnp.float32)
    query = rope(jnp.dot(tokens, w_query, preferred_element_type=jnp.float32), positions, pair_query).astype(jnp.bfloat16)
    key_proj = rope(jnp.dot(tokens, key_weight, preferred_element_type=jnp.float32), positions, partner_key).astype(jnp.bfloat16)
    value_proj = jnp.dot(tokens, value_weight, preferred_element_type=jnp.float32).astype(jnp.bfloat16)
    key_length = length_slot[slot_of]
    ancestral = strict_slot[slot_of[:, None], slot_of[None, :]] > 0.5
    visible = (ancestral & (index_real[None, :] < key_length[None, :])) | ((slot_of[:, None] == slot_of[None, :]) & (index_of[None, :] <= index_of[:, None]))
    group_width = QUERY_HEADS // KEY_VALUE_HEADS

    def one_head(head_index):
        head_query = lax.dynamic_slice_in_dim(query, head_index * HEAD_SIZE, HEAD_SIZE, 1)
        kv_start = (head_index // group_width) * HEAD_SIZE
        head_key = lax.dynamic_slice_in_dim(key_proj, kv_start, HEAD_SIZE, 1)
        head_value = lax.dynamic_slice_in_dim(value_proj, kv_start, HEAD_SIZE, 1)
        scores = jnp.dot(head_query, head_key.T, preferred_element_type=jnp.float32) * (HEAD_SIZE ** -0.5)
        peak_score = jnp.max(jnp.where(visible, scores, -jnp.inf), axis=1, keepdims=True)
        weights = jnp.where(visible, jnp.exp(scores - peak_score), 0.0)
        denominator = jnp.sum(weights, axis=1, keepdims=True)
        mixed = (jnp.dot(weights.astype(jnp.bfloat16), head_value, preferred_element_type=jnp.float32) / denominator).astype(jnp.bfloat16)
        readout = lax.dynamic_slice_in_dim(head_readout, head_index * HEAD_SIZE, HEAD_SIZE, 0)
        return jnp.dot(mixed, readout, preferred_element_type=jnp.float32)

    partials = lax.map(one_head, jnp.arange(QUERY_HEADS, dtype=jnp.int32))
    head_total = jnp.sum(partials, axis=0)
    residual = jnp.dot(tokens, resid_head, preferred_element_type=jnp.float32)
    live_mask = index_real < key_length
    token_values = jnp.where(live_mask, residual + head_total, 0.0)
    last_mask = index_real == key_length - 1.0
    leaf_per_slot = jnp.sum(jnp.where(last_mask, token_values, 0.0).reshape(SEGS, SEG_LEN), axis=1) * leaf_slot
    leaf_seg = jnp.dot(placement.T, leaf_per_slot, precision=lax.Precision.HIGHEST)
    backed = jnp.dot(ancestry.T, leaf_seg, precision=lax.Precision.HIGHEST) / jnp.dot(ancestry.T, leafy, precision=lax.Precision.HIGHEST)
    return token_values, backed
```

```python
import jax
import jax.numpy as jnp
from jax import lax
from jax.experimental import pallas as pl
from jax.experimental.pallas import tpu as pltpu
from jax.sharding import Mesh
from jax.sharding import PartitionSpec as P

KEY_VALUE_HEADS = 4
HEAD_SIZE = 128
ROPE_BASE = 1000000.0
SEG = ("y", "zl", "c")
FSDP = ("zh", "x")
META = 72
VMEM_LIMIT = 40 * 1024 * 1024

VMEM_SPEC = pl.BlockSpec(memory_space=pltpu.VMEM)
SMEM_SPEC = pl.BlockSpec(memory_space=pltpu.SMEM)


def tree_kernel(seg_ref, parents_ref, placed_ref, lengths_ref, meta_ref, table_ref, slot_of):
    segments = parents_ref.shape[0]
    slot = seg_ref[0]
    own = placed_ref[slot]

    def place(j, carry):
        slot_of[placed_ref[j]] = j
        return carry

    lax.fori_loop(0, segments, place, 0)

    def clear(j, carry):
        meta_ref[j] = 0
        return carry

    lax.fori_loop(0, META, clear, 0)

    def above(state):
        seg, count, offset = state
        meta_ref[8 + count] = slot_of[seg]
        meta_ref[40 + count] = lengths_ref[seg]
        return parents_ref[seg], count + 1, offset + lengths_ref[seg]

    _, count, offset = lax.while_loop(
        lambda state: state[0] >= 0, above, (parents_ref[own], jnp.int32(0), jnp.int32(0))
    )
    meta_ref[0] = count
    meta_ref[1] = offset
    meta_ref[2] = lengths_ref[own]

    row = lax.broadcasted_iota(jnp.int32, (128, 128), 0)
    col = lax.broadcasted_iota(jnp.int32, (128, 128), 1)
    row_s = lax.broadcasted_iota(jnp.int32, (segments, 128), 0)
    col_s = lax.broadcasted_iota(jnp.int32, (segments, 128), 1)
    parent_of = jnp.full((segments, 128), -1, jnp.int32)
    held = jnp.full((segments, 128), -1, jnp.int32)
    for i in range(segments):
        parent_of = jnp.where(row_s == i, parents_ref[i], parent_of)
        held = jnp.where(row_s == i, placed_ref[i], held)
    step = jnp.where(parent_of == col_s, 1.0, 0.0)
    step = jnp.concatenate([step, jnp.zeros((128 - segments, 128), jnp.float32)], axis=0)
    ancestry = jnp.where(row == col, 1.0, 0.0) + step

    def times(a, b):
        return jnp.dot(
            a.astype(jnp.bfloat16), b.astype(jnp.bfloat16), preferred_element_type=jnp.float32
        )

    power = step
    reach = 1
    while 2 * reach <= segments:
        power = times(power, power)
        ancestry = ancestry + times(power, ancestry)
        reach *= 2
    children = jnp.sum(step, axis=0, keepdims=True)
    leafy = jnp.where((children < 0.5) & (col[:1] < segments), 1.0, 0.0)
    leaves = times(jnp.broadcast_to(leafy, (8, 128)), ancestry)[:1]
    placement = jnp.where(held == col_s, 1.0, 0.0)
    share = times(placement * leafy, ancestry)
    table_ref[...] = jnp.where(col_s < segments, share / jnp.maximum(leaves, 1.0), 0.0)


def weights_kernel(seg_ref, value_ref, readout_ref, key_ref, resid_ref, out_ref):
    quarters, part, rows = value_ref.shape
    value = value_ref[...].reshape(quarters * part, rows)
    folded = jnp.dot(readout_ref[...], value, preferred_element_type=jnp.float32)
    heads = readout_ref.shape[0]
    high = folded.astype(jnp.bfloat16).astype(jnp.float32)
    low = folded - high
    start = pl.multiple_of(seg_ref[0] * rows, 128)
    resid = resid_ref[:, pl.ds(start, rows)].astype(jnp.float32)
    pad = jnp.zeros((7 - 2 * heads, rows), jnp.float32)
    piece = jnp.concatenate([high, low, resid, pad], axis=0)
    piece = jnp.concatenate([key_ref[...].astype(jnp.float32), piece], axis=0).astype(jnp.bfloat16)
    for i in range(out_ref.shape[0]):
        out_ref[i] = piece


def turned(raw, cosine, sine, axis):
    extent = raw.shape[axis]
    index = lax.broadcasted_iota(jnp.int32, raw.shape, axis)
    after = pltpu.roll(raw, extent - 1, axis)
    before = pltpu.roll(raw, 1, axis)
    return raw * cosine + jnp.where(index % 2 == 0, after, before) * sine


def keys_kernel(
    quarter_ref, tokens_ref, weights_ref, cosine_ref, sine_ref, out_ref, resid_ref, total
):
    step = pl.program_id(0)
    chunks, _, depth = weights_ref.shape

    @pl.when(step == 0)
    def _():
        total[...] = jnp.zeros_like(total)

    acc = total[...]
    for i in range(chunks):
        acc += lax.dot_general(
            weights_ref[i],
            tokens_ref[:, i * depth : (i + 1) * depth],
            (((1,), (1,)), ((), ())),
            preferred_element_type=jnp.float32,
        )
    total[...] = acc

    @pl.when(step == pl.num_programs(0) - 1)
    def _():
        width = total.shape[0] - 8
        start = pl.multiple_of(quarter_ref[0] * width, width)
        raw = total[:width]
        keys = turned(raw, cosine_ref[pl.ds(start, width)], sine_ref[pl.ds(start, width)], 0)
        last = total[width:]
        row = lax.broadcasted_iota(jnp.int32, last.shape, 0)
        summed = last + pltpu.roll(last, 6, 0)
        high = summed.astype(jnp.bfloat16).astype(jnp.float32)
        low = pltpu.roll(summed - high, 2, 0)
        tail = jnp.where(row < 2, high, jnp.where(row < 4, low, 0.0))
        piece = jnp.concatenate([keys, tail], axis=0).astype(jnp.bfloat16)
        for i in range(out_ref.shape[0]):
            out_ref[i] = piece
        resid_ref[...] = last[4:5]


def attention_kernel(
    place_ref,
    meta_ref,
    query_ref,
    cosine_ref,
    sine_ref,
    near_ref,
    far_ref,
    near_value_ref,
    far_value_ref,
    out_ref,
    query_buf,
    top,
    bottom,
    summed,
):
    seg_len = query_ref.shape[0]
    heads = query_ref.shape[1] // HEAD_SIZE
    own = place_ref[0]
    core = place_ref[1]
    raw = query_ref[...].T
    for h in range(heads):
        query_buf[h] = turned(
            raw[h * HEAD_SIZE : (h + 1) * HEAD_SIZE], cosine_ref[...], sine_ref[...], 0
        ).astype(jnp.bfloat16)
    scale = HEAD_SIZE ** (-0.5)
    key_at = lax.broadcasted_iota(jnp.int32, (seg_len, seg_len), 0)
    query_at = lax.broadcasted_iota(jnp.int32, (seg_len, seg_len), 1)

    def scores(keys, h):
        return scale * lax.dot_general(
            keys, query_buf[h], (((0,), (0,)), ((), ())), preferred_element_type=jnp.float32
        )

    own_keys = near_ref[:, own // 2].reshape(HEAD_SIZE, seg_len)
    own_values = near_value_ref[own // 2]
    for h in range(heads):
        masked = jnp.where(key_at <= query_at, scores(own_keys, h), -1e30)
        peak = jnp.max(masked, axis=0, keepdims=True)
        weights = jnp.where(key_at <= query_at, jnp.exp(masked - peak), 0.0)
        top[h] = peak
        bottom[h] = jnp.sum(weights, axis=0, keepdims=True)
        summed[h] = jnp.dot(
            own_values, weights.astype(jnp.bfloat16), preferred_element_type=jnp.float32
        )

    def visit(n, key_source, value_source):
        slot = meta_ref[8 + n]
        length = meta_ref[40 + n]
        keys = key_source[:, slot // 2].reshape(HEAD_SIZE, seg_len)
        values = value_source[slot // 2]
        for h in range(heads):
            masked = jnp.where(key_at < length, scores(keys, h), -1e30)
            peak = jnp.maximum(top[h], jnp.max(masked, axis=0, keepdims=True))
            shrink = jnp.exp(top[h] - peak)
            weights = jnp.where(key_at < length, jnp.exp(masked - peak), 0.0)
            top[h] = peak
            bottom[h] = bottom[h] * shrink + jnp.sum(weights, axis=0, keepdims=True)
            summed[h] = summed[h] * shrink + jnp.dot(
                values, weights.astype(jnp.bfloat16), preferred_element_type=jnp.float32
            )

    def one(n, carry):
        @pl.when(meta_ref[8 + n] % 2 == core)
        def _():
            visit(n, near_ref, near_value_ref)

        @pl.when(meta_ref[8 + n] % 2 != core)
        def _():
            visit(n, far_ref, far_value_ref)

        return carry

    lax.fori_loop(0, meta_ref[0], one, 0)
    result = jnp.zeros((1, seg_len), jnp.float32)
    for h in range(heads):
        both = summed[h]
        result += (both[h : h + 1] + both[2 + h : 3 + h]) / bottom[h]
    for i in range(out_ref.shape[0]):
        out_ref[i : i + 1] = result


def finish_kernel(meta_ref, parts_ref, resid_ref, out_ref, leaf_ref):
    total = resid_ref[...] + jnp.sum(parts_ref[...], axis=0, keepdims=True)
    index = lax.broadcasted_iota(jnp.int32, total.shape, 1)
    length = meta_ref[2]
    values = jnp.where(index < length, total, 0.0)
    out_ref[...] = values
    leaf = jnp.sum(jnp.where(index == length - 1, values, 0.0), axis=1, keepdims=True)
    leaf_ref[...] = jnp.broadcast_to(leaf, leaf_ref.shape)


def gathered(value, axis):
    return lax.all_to_all(value, axis, 0, 0)


def on_device(
    tokens, w_query, key_weight, value_weight, resid_head, head_readout, parents, placed, lengths
):
    seg_len, model_width = tokens.shape
    seg_index = lax.axis_index(SEG).astype(jnp.int32)
    quarter = lax.axis_index("x").astype(jnp.int32)
    core = lax.axis_index("c").astype(jnp.int32)
    segments = parents.shape[0]
    fsdp_size = lax.axis_size(FSDP)
    quarters = lax.axis_size("x")
    pairs = segments // 2
    width = key_weight.shape[1]
    heads = w_query.shape[1] // HEAD_SIZE
    params = pltpu.CompilerParams(vmem_limit_bytes=VMEM_LIMIT)

    query_weight = lax.all_gather(w_query, SEG, axis=0, tiled=True)

    meta, table = pl.pallas_call(
        tree_kernel,
        out_shape=(
            jax.ShapeDtypeStruct((META,), jnp.int32),
            jax.ShapeDtypeStruct((segments, 128), jnp.float32),
        ),
        in_specs=[SMEM_SPEC] * 4,
        out_specs=(SMEM_SPEC, VMEM_SPEC),
        scratch_shapes=[pltpu.SMEM((segments,), jnp.int32)],
        compiler_params=params,
        name="tree",
    )(seg_index.reshape(1), parents, placed, lengths)

    positions = meta[1].astype(jnp.float32) + jnp.arange(seg_len, dtype=jnp.float32)
    dims = jnp.arange(HEAD_SIZE, dtype=jnp.int32)
    frequency = ROPE_BASE ** (-2.0 * (dims // 2).astype(jnp.float32) / HEAD_SIZE)
    angles = frequency[:, None] * positions[None, :]
    cosine = jnp.cos(angles)
    sine = jnp.sin(angles) * jnp.where(dims % 2 == 0, -1.0, 1.0)[:, None]

    values_x = gathered(jnp.broadcast_to(value_weight.T[None], (quarters, width, seg_len)), "x")
    rows = width + 8
    pieces = pl.pallas_call(
        weights_kernel,
        out_shape=jax.ShapeDtypeStruct((segments, rows, seg_len), jnp.bfloat16),
        in_specs=[SMEM_SPEC] + [VMEM_SPEC] * 4,
        out_specs=VMEM_SPEC,
        compiler_params=params,
        name="fold_weights",
    )(
        seg_index.reshape(1),
        values_x,
        head_readout.reshape(heads, HEAD_SIZE),
        key_weight.T,
        resid_head.reshape(1, model_width),
    )
    key_weights = gathered(pieces, SEG)

    steps = 8
    keys, residual = pl.pallas_call(
        keys_kernel,
        out_shape=(
            jax.ShapeDtypeStruct((pairs, rows, seg_len), jnp.bfloat16),
            jax.ShapeDtypeStruct((1, seg_len), jnp.float32),
        ),
        grid=(steps,),
        in_specs=[
            SMEM_SPEC,
            pl.BlockSpec((seg_len, model_width // steps), lambda k: (0, k)),
            pl.BlockSpec((segments // steps, rows, seg_len), lambda k: (k, 0, 0)),
            pl.BlockSpec((HEAD_SIZE, seg_len), lambda k: (0, 0)),
            pl.BlockSpec((HEAD_SIZE, seg_len), lambda k: (0, 0)),
        ],
        out_specs=(
            pl.BlockSpec((pairs, rows, seg_len), lambda k: (0, 0, 0)),
            pl.BlockSpec((1, seg_len), lambda k: (0, 0)),
        ),
        scratch_shapes=[pltpu.VMEM((rows, seg_len), jnp.float32)],
        compiler_params=params,
        name="project_keys",
    )(quarter.reshape(1), tokens, key_weights, cosine, sine)

    keys_yz = gathered(keys, ("y", "zl"))
    near_values = keys_yz[:, width:]
    swap = [(0, 1), (1, 0)]
    far_values = lax.ppermute(near_values, "c", swap)
    near = gathered(
        jnp.broadcast_to(keys_yz[None, :, :width], (quarters, pairs, width, seg_len)), "x"
    )
    far = lax.ppermute(near, "c", swap)

    query_raw = jnp.dot(tokens, query_weight, preferred_element_type=jnp.float32)
    mixed = pl.pallas_call(
        attention_kernel,
        out_shape=jax.ShapeDtypeStruct((fsdp_size, seg_len), jnp.float32),
        in_specs=[SMEM_SPEC] * 2 + [VMEM_SPEC] * 7,
        out_specs=VMEM_SPEC,
        scratch_shapes=[
            pltpu.VMEM((heads, HEAD_SIZE, seg_len), jnp.bfloat16),
            pltpu.VMEM((heads, 1, seg_len), jnp.float32),
            pltpu.VMEM((heads, 1, seg_len), jnp.float32),
            pltpu.VMEM((heads, 8, seg_len), jnp.float32),
        ],
        compiler_params=params,
        name="attend",
    )(
        jnp.stack([seg_index, core]),
        meta,
        query_raw,
        cosine,
        sine,
        near,
        far,
        near_values,
        far_values,
    )
    parts = gathered(mixed, FSDP)
    token_values, leaf_rows = pl.pallas_call(
        finish_kernel,
        out_shape=(
            jax.ShapeDtypeStruct((1, seg_len), jnp.float32),
            jax.ShapeDtypeStruct((segments, 128), jnp.float32),
        ),
        in_specs=[SMEM_SPEC, VMEM_SPEC, VMEM_SPEC],
        out_specs=(VMEM_SPEC, VMEM_SPEC),
        compiler_params=params,
        name="token_values",
    )(meta, parts, residual)
    leaves = gathered(leaf_rows, SEG)
    branch = jnp.sum(leaves * table, axis=0)[:segments]
    return (token_values.reshape(seg_len), branch)


def solution(mesh):
    fine = Mesh(mesh.devices.reshape(8, 2, 2, 4, 4), SEG + FSDP)
    in_specs = (
        P(SEG, None),
        P(SEG, FSDP),
        P(SEG, FSDP),
        P(SEG, FSDP),
        P(),
        P(FSDP),
        P(),
        P(),
        P(),
    )
    out_specs = (P(SEG), P())
    return jax.shard_map(
        on_device, mesh=fine, in_specs=in_specs, out_specs=out_specs, check_vma=False
    )
```

```python
import jax
import jax.numpy as jnp
from jax import lax
from jax.experimental import pallas as pl
from jax.experimental.pallas import tpu as pltpu
from jax.sharding import Mesh
from jax.sharding import PartitionSpec as P

KEY_VALUE_HEADS = 4
HEAD_SIZE = 128
ROPE_BASE = 1000000.0
SEG = ("y", "zl", "c")
FSDP = ("zh", "x")
NEAR, FAR, LENGTHS, META = 8, 48, 80, 168
VMEM_LIMIT = 40 * 1024 * 1024

VMEM_SPEC = pl.BlockSpec(memory_space=pltpu.VMEM)
SMEM_SPEC = pl.BlockSpec(memory_space=pltpu.SMEM)
HBM_SPEC = pl.BlockSpec(memory_space=pltpu.HBM)


def tree_kernel(
    parents_src,
    placed_src,
    lengths_src,
    meta_ref,
    table_ref,
    position_ref,
    parents_ref,
    placed_ref,
    lengths_ref,
    slot_of,
    sems,
):
    copies = [
        pltpu.make_async_copy(source, there, sems.at[i])
        for i, (source, there) in enumerate(
            ((parents_src, parents_ref), (placed_src, placed_ref), (lengths_src, lengths_ref))
        )
    ]
    for copy in copies:
        copy.start()
    for copy in copies:
        copy.wait()
    segments = parents_ref.shape[0]
    slot = lax.axis_index(SEG)
    own = placed_ref[slot]

    def place(j, carry):
        slot_of[placed_ref[j]] = j
        return carry

    lax.fori_loop(0, segments, place, 0)

    def clear(j, carry):
        meta_ref[j] = 0
        return carry

    lax.fori_loop(0, META, clear, 0)

    def above(state):
        seg, near, far, offset = state
        there = slot_of[seg]
        is_near = (there % 2 == slot % 2).astype(jnp.int32)
        entry = jnp.where(is_near == 1, NEAR + near, FAR + far)
        meta_ref[entry] = there
        meta_ref[LENGTHS + entry] = lengths_ref[seg]
        return parents_ref[seg], near + is_near, far + 1 - is_near, offset + lengths_ref[seg]

    zero = jnp.int32(0)
    _, near, far, offset = lax.while_loop(
        lambda state: state[0] >= 0, above, (parents_ref[own], zero, zero, zero)
    )
    meta_ref[0] = near
    meta_ref[1] = far
    meta_ref[2] = lengths_ref[own]
    index = lax.broadcasted_iota(jnp.int32, position_ref.shape, 1)
    position_ref[...] = (offset + index).astype(jnp.float32)

    row = lax.broadcasted_iota(jnp.int32, (128, 128), 0)
    col = lax.broadcasted_iota(jnp.int32, (128, 128), 1)
    row_s = lax.broadcasted_iota(jnp.int32, (segments, 128), 0)
    col_s = lax.broadcasted_iota(jnp.int32, (segments, 128), 1)
    parent_of = jnp.full((segments, 128), -1, jnp.int32)
    held = jnp.full((segments, 128), -1, jnp.int32)
    for i in range(segments):
        parent_of = jnp.where(row_s == i, parents_ref[i], parent_of)
        held = jnp.where(row_s == i, placed_ref[i], held)
    step = jnp.where(parent_of == col_s, 1.0, 0.0)
    step = jnp.concatenate([step, jnp.zeros((128 - segments, 128), jnp.float32)], axis=0)
    ancestry = jnp.where(row == col, 1.0, 0.0) + step

    def times(a, b):
        return jnp.dot(
            a.astype(jnp.bfloat16), b.astype(jnp.bfloat16), preferred_element_type=jnp.float32
        )

    power = step
    reach = 1
    while 2 * reach <= segments:
        power = times(power, power)
        ancestry = ancestry + times(power, ancestry)
        reach *= 2
    children = jnp.sum(step, axis=0, keepdims=True)
    leafy = jnp.where((children < 0.5) & (col[:1] < segments), 1.0, 0.0)
    leaves = times(jnp.broadcast_to(leafy, (8, 128)), ancestry)[:1]
    placement = jnp.where(held == col_s, 1.0, 0.0)
    share = times(placement * leafy, ancestry)
    table_ref[...] = jnp.where(col_s < segments, share / jnp.maximum(leaves, 1.0), 0.0)


def weights_kernel(value_ref, readout_ref, key_ref, out_ref):
    quarters, part, rows = value_ref.shape
    value = value_ref[...].reshape(quarters * part, rows)
    readout = readout_ref[...].astype(jnp.bfloat16)
    folded = jnp.dot(readout, value, preferred_element_type=jnp.float32)
    heads = readout_ref.shape[0]
    high = folded.astype(jnp.bfloat16).astype(jnp.float32)
    low = folded - high
    pad = jnp.zeros((8 - 2 * heads, rows), jnp.float32)
    piece = jnp.concatenate([key_ref[...], high, low, pad], axis=0).astype(jnp.bfloat16)
    for i in range(out_ref.shape[0]):
        out_ref[i] = piece


def turned(raw, cosine, sine, axis):
    extent = raw.shape[axis]
    index = lax.broadcasted_iota(jnp.int32, raw.shape, axis)
    after = pltpu.roll(raw, extent - 1, axis)
    before = pltpu.roll(raw, 1, axis)
    return raw * cosine + jnp.where(index % 2 == 0, after, before) * sine


def half_projected(tokens_ref, weights_ref, total, parity):
    for even in range(2):

        @pl.when(parity == even)
        def _():
            blocks, _, depth = weights_ref.shape
            acc = total[...]
            for p in range(blocks):
                start = (2 * p + even) * depth
                acc += lax.dot_general(
                    weights_ref[p],
                    tokens_ref[:, start : start + depth],
                    (((1,), (1,)), ((), ())),
                    preferred_element_type=jnp.float32,
                )
            total[...] = acc


def near_keys_kernel(tokens_ref, weights_ref, out_ref):
    out_ref[...] = jnp.zeros_like(out_ref)
    half_projected(tokens_ref, weights_ref, out_ref, lax.axis_index("c"))


def far_keys_kernel(
    tokens_ref, weights_ref, near_ref, cosine_ref, sine_ref, out_ref, total
):
    total[...] = near_ref[...]
    half_projected(tokens_ref, weights_ref, total, 1 - lax.axis_index("c"))
    width = total.shape[0] - 8
    start = pl.multiple_of(lax.axis_index("x") * width, width)
    keys = turned(total[:width], cosine_ref[pl.ds(start, width)], sine_ref[pl.ds(start, width)], 0)
    last = total[width:]
    row = lax.broadcasted_iota(jnp.int32, last.shape, 0)
    summed = last + pltpu.roll(last, 6, 0)
    high = summed.astype(jnp.bfloat16).astype(jnp.float32)
    low = pltpu.roll(summed - high, 2, 0)
    tail = jnp.where(row < 2, high, jnp.where(row < 4, low, 0.0))
    piece = jnp.concatenate([keys, tail], axis=0).astype(jnp.bfloat16)
    for i in range(out_ref.shape[0]):
        out_ref[i] = piece


def queries_kernel(
    tokens_ref, weights_ref, readout_ref, cosine_ref, sine_ref, out_ref, resid_ref, total
):
    readout = jnp.broadcast_to(readout_ref[...], (8, readout_ref.shape[1]))
    resid_ref[...] = lax.dot_general(
        readout.astype(jnp.bfloat16),
        tokens_ref[...],
        (((1,), (1,)), ((), ())),
        preferred_element_type=jnp.float32,
    )[:1]
    blocks, depth, _ = weights_ref.shape
    seg_len = tokens_ref.shape[0]
    half = lax.axis_index("zl")
    for upper in range(2):

        @pl.when(half == upper)
        def _():
            acc = jnp.zeros_like(total)
            for i in range(blocks):
                block = i // 4 * 4 + (i % 2 ^ upper) * 2 + i // 2 % 2
                acc += jnp.dot(
                    tokens_ref[:, block * depth : (block + 1) * depth],
                    weights_ref[i],
                    preferred_element_type=jnp.float32,
                )
            total[...] = acc

    raw = total[...].T
    for h in range(raw.shape[0] // HEAD_SIZE):
        head = raw[h * HEAD_SIZE : (h + 1) * HEAD_SIZE]
        out_ref[:, h * seg_len : (h + 1) * seg_len] = turned(
            head, cosine_ref[...], sine_ref[...], 0
        ).astype(jnp.bfloat16)


def attention_kernel(meta_ref, query_ref, near_ref, far_ref, out_ref, top, bottom, summed):
    seg_len = near_ref.shape[3]
    columns = query_ref.shape[1]
    heads = columns // seg_len
    own = lax.axis_index(SEG)
    quarter = lax.axis_index("x")
    quarters = lax.axis_size("x")
    width = HEAD_SIZE // quarters
    scale = HEAD_SIZE ** (-0.5)
    key_at = lax.broadcasted_iota(jnp.int32, (seg_len, columns), 0)
    query_at = lax.broadcasted_iota(jnp.int32, (seg_len, columns), 1) % seg_len

    def scores(source, slot, seen):
        keys = source[pl.ds(slot // 2 % 2 * quarters, quarters), slot // 4, :width]
        raw = lax.dot_general(
            keys.reshape(HEAD_SIZE, seg_len),
            query_ref[...],
            (((0,), (0,)), ((), ())),
            preferred_element_type=jnp.float32,
        )
        return jnp.where(seen, raw * scale, -1e30)

    def mix(source, slot, weights):
        piece = source[slot // 2 % 2 * quarters + quarter, slot // 4].astype(jnp.float32)
        return jnp.dot(
            piece[width:].astype(jnp.bfloat16),
            weights.astype(jnp.bfloat16),
            preferred_element_type=jnp.float32,
        )

    masked = scores(near_ref, own, key_at <= query_at)
    peak = jnp.max(masked, axis=0, keepdims=True)
    weights = jnp.exp(masked - peak)
    top[...] = peak
    bottom[...] = jnp.sum(weights, axis=0, keepdims=True)
    summed[...] = mix(near_ref, own, weights)

    def visit_two(entry, source):
        slots = [meta_ref[entry + i] for i in range(2)]
        masked = [
            scores(source, slots[i], key_at < meta_ref[LENGTHS + entry + i]) for i in range(2)
        ]
        peak = jnp.max(jnp.maximum(masked[0], masked[1]), axis=0, keepdims=True)
        peak = jnp.maximum(top[...], peak)
        shrink = jnp.exp(top[...] - peak)
        weights = [jnp.exp(m - peak) for m in masked]
        top[...] = peak
        bottom[...] = bottom[...] * shrink + jnp.sum(
            weights[0] + weights[1], axis=0, keepdims=True
        )
        summed[...] = (
            summed[...] * shrink
            + mix(source, slots[0], weights[0])
            + mix(source, slots[1], weights[1])
        )

    def near_two(n, carry):
        visit_two(NEAR + 2 * n, near_ref)
        return carry

    def far_two(n, carry):
        visit_two(FAR + 2 * n, far_ref)
        return carry

    lax.fori_loop(0, (meta_ref[0] + 1) // 2, near_two, 0)
    lax.fori_loop(0, (meta_ref[1] + 1) // 2, far_two, 0)
    scaled = summed[...] / bottom[...]
    result = jnp.zeros((1, seg_len), jnp.float32)
    for h in range(heads):
        part = scaled[:, h * seg_len : (h + 1) * seg_len]
        result += part[h : h + 1] + part[2 + h : 3 + h]
    for i in range(out_ref.shape[0]):
        out_ref[i] = jnp.broadcast_to(result, out_ref.shape[1:])


def finish_kernel(meta_ref, parts_ref, resid_ref, out_ref, leaf_ref):
    total = resid_ref[...] + jnp.sum(parts_ref[...], axis=0)[:1]
    index = lax.broadcasted_iota(jnp.int32, total.shape, 1)
    length = meta_ref[2]
    values = jnp.where(index < length, total, 0.0)
    out_ref[...] = values
    leaf = jnp.sum(jnp.where(index == length - 1, values, 0.0), axis=1, keepdims=True)
    leaf_ref[...] = jnp.broadcast_to(leaf, leaf_ref.shape)


def gathered(value, axis):
    return lax.all_to_all(value, axis, 0, 0)


def on_device(
    tokens, w_query, key_weight, value_weight, resid_head, head_readout, parents, placed, lengths
):
    seg_len, model_width = tokens.shape
    segments = parents.shape[0]
    fsdp_size = lax.axis_size(FSDP)
    quarters = lax.axis_size("x")
    pairs = segments // 2
    width = key_weight.shape[1]
    rows = width + 8
    heads = w_query.shape[1] // HEAD_SIZE
    swap = [(0, 1), (1, 0)]
    params = pltpu.CompilerParams(vmem_limit_bytes=VMEM_LIMIT)

    other = lax.ppermute(w_query, "zl", swap)
    values_x = gathered(jnp.broadcast_to(value_weight.T[None], (quarters, width, seg_len)), "x")
    readout = head_readout.reshape(heads, HEAD_SIZE).astype(jnp.float32)
    key_rows = key_weight.T.astype(jnp.float32)
    values_x, other, readout, key_rows = lax.optimization_barrier(
        (values_x, other, readout, key_rows)
    )
    query_weight = lax.all_gather(
        jnp.concatenate([w_query, other]), ("y", "c"), axis=0, tiled=True
    )
    pieces = pl.pallas_call(
        weights_kernel,
        out_shape=jax.ShapeDtypeStruct((pairs, rows, seg_len), jnp.bfloat16),
        in_specs=[VMEM_SPEC] * 3,
        out_specs=VMEM_SPEC,
        compiler_params=params,
        name="fold_weights",
    )(values_x, readout, key_rows)

    near_weights = gathered(pieces, ("y", "zl"))
    meta, table, positions = pl.pallas_call(
        tree_kernel,
        out_shape=(
            jax.ShapeDtypeStruct((META,), jnp.int32),
            jax.ShapeDtypeStruct((segments, 128), jnp.float32),
            jax.ShapeDtypeStruct((1, seg_len), jnp.float32),
        ),
        in_specs=[HBM_SPEC] * 3,
        out_specs=(SMEM_SPEC, VMEM_SPEC, VMEM_SPEC),
        scratch_shapes=[pltpu.SMEM((segments,), jnp.int32)] * 4
        + [pltpu.SemaphoreType.DMA((3,))],
        compiler_params=params,
        name="tree",
    )(parents, placed, lengths)
    dims = jnp.arange(HEAD_SIZE, dtype=jnp.int32)
    frequency = ROPE_BASE ** (-2.0 * (dims // 2).astype(jnp.float32) / HEAD_SIZE)
    angles = frequency[:, None] * positions
    cosine = jnp.cos(angles)
    sine = jnp.sin(angles) * jnp.where(dims % 2 == 0, -1.0, 1.0)[:, None]
    readout_row = resid_head.reshape(1, model_width).astype(jnp.float32)
    near_weights, cosine, sine, readout_row = lax.optimization_barrier(
        (near_weights, cosine, sine, readout_row)
    )

    far_weights = lax.ppermute(near_weights, "c", swap)
    near_sums = pl.pallas_call(
        near_keys_kernel,
        out_shape=jax.ShapeDtypeStruct((rows, seg_len), jnp.float32),
        in_specs=[VMEM_SPEC] * 2,
        out_specs=VMEM_SPEC,
        compiler_params=params,
        cost_estimate=pl.CostEstimate(
            flops=rows * seg_len * model_width, bytes_accessed=2**21, transcendentals=0
        ),
        name="project_near_keys",
    )(tokens, near_weights)
    far_weights, near_sums = lax.optimization_barrier((far_weights, near_sums))
    keys = pl.pallas_call(
        far_keys_kernel,
        out_shape=jax.ShapeDtypeStruct((lax.axis_size("y"), rows, seg_len), jnp.bfloat16),
        in_specs=[VMEM_SPEC] * 5,
        out_specs=VMEM_SPEC,
        scratch_shapes=[pltpu.VMEM((rows, seg_len), jnp.float32)],
        compiler_params=params,
        name="project_far_keys",
    )(tokens, far_weights, near_sums, cosine, sine)

    keys_y = gathered(keys, "y")
    spread = lax.axis_size(("zl", "x"))
    near = gathered(jnp.broadcast_to(keys_y[None], (spread, *keys_y.shape)), ("zl", "x"))
    queries, residual = pl.pallas_call(
        queries_kernel,
        out_shape=(
            jax.ShapeDtypeStruct((HEAD_SIZE, heads * seg_len), jnp.bfloat16),
            jax.ShapeDtypeStruct((1, seg_len), jnp.float32),
        ),
        in_specs=[VMEM_SPEC] * 5,
        out_specs=(VMEM_SPEC, VMEM_SPEC),
        scratch_shapes=[pltpu.VMEM((seg_len, heads * HEAD_SIZE), jnp.float32)],
        cost_estimate=pl.CostEstimate(
            flops=2 * seg_len * model_width * heads * HEAD_SIZE,
            bytes_accessed=2 * model_width * (seg_len + heads * HEAD_SIZE),
            transcendentals=0,
        ),
        compiler_params=params,
        name="project_queries",
    )(
        tokens,
        query_weight.reshape(segments, seg_len, -1),
        readout_row,
        cosine,
        sine,
    )
    near, queries = lax.optimization_barrier((near, queries))
    far = lax.ppermute(near, "c", swap)
    mixed = pl.pallas_call(
        attention_kernel,
        out_shape=jax.ShapeDtypeStruct((fsdp_size, 8, seg_len), jnp.float32),
        in_specs=[SMEM_SPEC] + [VMEM_SPEC] * 3,
        out_specs=VMEM_SPEC,
        scratch_shapes=[
            pltpu.VMEM((1, heads * seg_len), jnp.float32),
            pltpu.VMEM((1, heads * seg_len), jnp.float32),
            pltpu.VMEM((8, heads * seg_len), jnp.float32),
        ],
        compiler_params=params,
        name="attend",
    )(meta, queries, near, far)
    parts = gathered(mixed, FSDP)
    token_values, leaf_rows = pl.pallas_call(
        finish_kernel,
        out_shape=(
            jax.ShapeDtypeStruct((1, seg_len), jnp.float32),
            jax.ShapeDtypeStruct((segments, 128), jnp.float32),
        ),
        in_specs=[SMEM_SPEC, VMEM_SPEC, VMEM_SPEC],
        out_specs=(VMEM_SPEC, VMEM_SPEC),
        compiler_params=params,
        name="token_values",
    )(meta, parts, residual)
    leaves = gathered(leaf_rows, SEG)
    branch = jnp.sum(leaves * table, axis=0)[:segments]
    return (token_values.reshape(seg_len), branch)


def solution(mesh):
    fine = Mesh(mesh.devices.reshape(8, 2, 2, 4, 4), SEG + FSDP)
    in_specs = (
        P(SEG, None),
        P(SEG, FSDP),
        P(SEG, FSDP),
        P(SEG, FSDP),
        P(),
        P(FSDP),
        P(),
        P(),
        P(),
    )
    out_specs = (P(SEG), P())
    return jax.shard_map(
        on_device, mesh=fine, in_specs=in_specs, out_specs=out_specs, check_vma=False
    )
```

```python
import jax
import jax.numpy as jnp
from jax import lax
from jax.experimental import pallas as pl
from jax.experimental.pallas import tpu as pltpu
from jax.sharding import Mesh
from jax.sharding import PartitionSpec as P

KEY_VALUE_HEADS = 4
HEAD_SIZE = 128
ROPE_BASE = 1000000.0
SEG = ("y", "zl", "c")
FSDP = ("zh", "x")
NEAR, FAR, LENGTHS, META = 8, 48, 80, 168
VMEM_LIMIT = 40 * 1024 * 1024

VMEM_SPEC = pl.BlockSpec(memory_space=pltpu.VMEM)
SMEM_SPEC = pl.BlockSpec(memory_space=pltpu.SMEM)
HBM_SPEC = pl.BlockSpec(memory_space=pltpu.HBM)


def tree_kernel(
    parents_src,
    placed_src,
    lengths_src,
    meta_ref,
    table_ref,
    position_ref,
    parents_ref,
    placed_ref,
    lengths_ref,
    slot_of,
    sems,
):
    copies = [
        pltpu.make_async_copy(source, there, sems.at[i])
        for i, (source, there) in enumerate(
            ((parents_src, parents_ref), (placed_src, placed_ref), (lengths_src, lengths_ref))
        )
    ]
    for copy in copies:
        copy.start()
    for copy in copies:
        copy.wait()
    segments = parents_ref.shape[0]
    slot = lax.axis_index(SEG)
    own = placed_ref[slot]

    def place(j, carry):
        slot_of[placed_ref[j]] = j
        return carry

    lax.fori_loop(0, segments, place, 0)

    def clear(j, carry):
        meta_ref[j] = 0
        return carry

    lax.fori_loop(0, META, clear, 0)

    def above(state):
        seg, near, far, offset = state
        there = slot_of[seg]
        is_near = (there % 2 == slot % 2).astype(jnp.int32)
        entry = jnp.where(is_near == 1, NEAR + near, FAR + far)
        meta_ref[entry] = there
        meta_ref[LENGTHS + entry] = lengths_ref[seg]
        return parents_ref[seg], near + is_near, far + 1 - is_near, offset + lengths_ref[seg]

    zero = jnp.int32(0)
    _, near, far, offset = lax.while_loop(
        lambda state: state[0] >= 0, above, (parents_ref[own], zero, zero, zero)
    )
    meta_ref[0] = near
    meta_ref[1] = far
    meta_ref[2] = lengths_ref[own]
    index = lax.broadcasted_iota(jnp.int32, position_ref.shape, 1)
    position_ref[...] = (offset + index).astype(jnp.float32)

    row = lax.broadcasted_iota(jnp.int32, (128, 128), 0)
    col = lax.broadcasted_iota(jnp.int32, (128, 128), 1)
    row_s = lax.broadcasted_iota(jnp.int32, (segments, 128), 0)
    col_s = lax.broadcasted_iota(jnp.int32, (segments, 128), 1)
    parent_of = jnp.full((segments, 128), -1, jnp.int32)
    held = jnp.full((segments, 128), -1, jnp.int32)
    for i in range(segments):
        parent_of = jnp.where(row_s == i, parents_ref[i], parent_of)
        held = jnp.where(row_s == i, placed_ref[i], held)
    step = jnp.where(parent_of == col_s, 1.0, 0.0)
    step = jnp.concatenate([step, jnp.zeros((128 - segments, 128), jnp.float32)], axis=0)
    ancestry = jnp.where(row == col, 1.0, 0.0) + step

    def times(a, b):
        return jnp.dot(
            a.astype(jnp.bfloat16), b.astype(jnp.bfloat16), preferred_element_type=jnp.float32
        )

    power = step
    reach = 1
    while 2 * reach <= segments:
        power = times(power, power)
        ancestry = ancestry + times(power, ancestry)
        reach *= 2
    children = jnp.sum(step, axis=0, keepdims=True)
    leafy = jnp.where((children < 0.5) & (col[:1] < segments), 1.0, 0.0)
    leaves = times(jnp.broadcast_to(leafy, (8, 128)), ancestry)[:1]
    placement = jnp.where(held == col_s, 1.0, 0.0)
    share = times(placement * leafy, ancestry)
    table_ref[...] = jnp.where(col_s < segments, share / jnp.maximum(leaves, 1.0), 0.0)


def weights_kernel(value_ref, readout_ref, key_ref, out_ref):
    quarters, part, rows = value_ref.shape
    value = value_ref[...].reshape(quarters * part, rows)
    readout = readout_ref[...].astype(jnp.bfloat16)
    folded = jnp.dot(readout, value, preferred_element_type=jnp.float32)
    high = folded.astype(jnp.bfloat16).astype(jnp.float32)
    low = folded - high
    width = key_ref.shape[0] - 8
    piece = jnp.concatenate([key_ref[:width], high, low, key_ref[width + 4 :]], axis=0)
    piece = piece.astype(jnp.bfloat16)
    for i in range(out_ref.shape[0]):
        out_ref[i] = piece


def turned(raw, cosine, sine, axis):
    extent = raw.shape[axis]
    index = lax.broadcasted_iota(jnp.int32, raw.shape, axis)
    after = pltpu.roll(raw, extent - 1, axis)
    before = pltpu.roll(raw, 1, axis)
    return raw * cosine + jnp.where(index % 2 == 0, after, before) * sine


def half_projected(tokens_ref, weights_ref, total, parity):
    for even in range(2):

        @pl.when(parity == even)
        def _():
            blocks, _, depth = weights_ref.shape
            acc = total[...]
            for p in range(blocks):
                start = (2 * p + even) * depth
                acc += lax.dot_general(
                    weights_ref[p],
                    tokens_ref[:, start : start + depth],
                    (((1,), (1,)), ((), ())),
                    preferred_element_type=jnp.float32,
                )
            total[...] = acc


def near_keys_kernel(tokens_ref, weights_ref, out_ref):
    out_ref[...] = jnp.zeros_like(out_ref)
    half_projected(tokens_ref, weights_ref, out_ref, lax.axis_index("c"))


def far_keys_kernel(
    tokens_ref, weights_ref, near_ref, cosine_ref, sine_ref, out_ref, resid_ref, total
):
    total[...] = near_ref[...]
    half_projected(tokens_ref, weights_ref, total, 1 - lax.axis_index("c"))
    width = total.shape[0] - 8
    start = pl.multiple_of(lax.axis_index("x") * width, width)
    keys = turned(total[:width], cosine_ref[pl.ds(start, width)], sine_ref[pl.ds(start, width)], 0)
    last = total[width:]
    row = lax.broadcasted_iota(jnp.int32, last.shape, 0)
    summed = last + pltpu.roll(last, 6, 0)
    high = summed.astype(jnp.bfloat16).astype(jnp.float32)
    low = pltpu.roll(summed - high, 2, 0)
    tail = jnp.where(row < 2, high, jnp.where(row < 4, low, 0.0))
    resid_ref[...] = last[4:5]
    piece = jnp.concatenate([keys, tail], axis=0).astype(jnp.bfloat16)
    for i in range(out_ref.shape[0]):
        out_ref[i] = piece


def queries_kernel(tokens_ref, weights_ref, cosine_ref, sine_ref, out_ref, total):
    blocks, depth, _ = weights_ref.shape
    seg_len = tokens_ref.shape[0]
    half = lax.axis_index("zl")
    for upper in range(2):

        @pl.when(half == upper)
        def _():
            acc = jnp.zeros_like(total)
            for i in range(blocks):
                block = i // 4 * 4 + (i % 2 ^ upper) * 2 + i // 2 % 2
                acc += jnp.dot(
                    tokens_ref[:, block * depth : (block + 1) * depth],
                    weights_ref[i],
                    preferred_element_type=jnp.float32,
                )
            total[...] = acc

    raw = total[...].T
    for h in range(raw.shape[0] // HEAD_SIZE):
        head = raw[h * HEAD_SIZE : (h + 1) * HEAD_SIZE]
        out_ref[:, h * seg_len : (h + 1) * seg_len] = turned(
            head, cosine_ref[...], sine_ref[...], 0
        ).astype(jnp.bfloat16)


def scored(query_ref, keys_ref, slot, seen):
    quarters = lax.axis_size("x")
    seg_len = keys_ref.shape[3]
    keys = keys_ref[pl.ds(slot // 2 % 2 * quarters, quarters), slot // 4]
    raw = lax.dot_general(
        keys.reshape(HEAD_SIZE, seg_len),
        query_ref[...],
        (((0,), (0,)), ((), ())),
        preferred_element_type=jnp.float32,
    )
    return jnp.where(seen, raw * HEAD_SIZE ** (-0.5), -1e30)


def mixed_values(own_ref, other_ref, far, slot, weights):
    is_other = slot // 2 % 2 != lax.axis_index("zl")
    own, other = (ref[far, slot // 4].astype(jnp.float32) for ref in (own_ref, other_ref))
    return jnp.dot(
        jnp.where(is_other, other, own).astype(jnp.bfloat16),
        weights.astype(jnp.bfloat16),
        preferred_element_type=jnp.float32,
    )


def visit(meta_ref, far, query_ref, keys_ref, own_ref, other_ref, top, bottom, summed):
    key_at = lax.broadcasted_iota(jnp.int32, (keys_ref.shape[3], query_ref.shape[1]), 0)
    first = (NEAR, FAR)[far]

    def two(n, carry):
        entries = [first + 2 * n, first + 2 * n + 1]
        slots = [meta_ref[e] for e in entries]
        masked = [
            scored(query_ref, keys_ref, slot, key_at < meta_ref[LENGTHS + e])
            for e, slot in zip(entries, slots)
        ]
        peak = jnp.max(jnp.maximum(masked[0], masked[1]), axis=0, keepdims=True)
        peak = jnp.maximum(top[...], peak)
        shrink = jnp.exp(top[...] - peak)
        weights = [jnp.exp(m - peak) for m in masked]
        top[...] = peak
        bottom[...] = bottom[...] * shrink + jnp.sum(
            weights[0] + weights[1], axis=0, keepdims=True
        )
        summed[...] = (
            summed[...] * shrink
            + mixed_values(own_ref, other_ref, far, slots[0], weights[0])
            + mixed_values(own_ref, other_ref, far, slots[1], weights[1])
        )
        return carry

    lax.fori_loop(0, (meta_ref[far] + 1) // 2, two, 0)


def near_kernel(meta_ref, query_ref, keys_ref, own_ref, other_ref, top, bottom, summed):
    seg_len = keys_ref.shape[3]
    shape = (seg_len, query_ref.shape[1])
    key_at = lax.broadcasted_iota(jnp.int32, shape, 0)
    query_at = lax.broadcasted_iota(jnp.int32, shape, 1) % seg_len
    own = lax.axis_index(SEG)
    masked = scored(query_ref, keys_ref, own, key_at <= query_at)
    peak = jnp.max(masked, axis=0, keepdims=True)
    weights = jnp.exp(masked - peak)
    top[...] = peak
    bottom[...] = jnp.sum(weights, axis=0, keepdims=True)
    summed[...] = mixed_values(own_ref, other_ref, 0, own, weights)
    visit(meta_ref, 0, query_ref, keys_ref, own_ref, other_ref, top, bottom, summed)


def far_kernel(
    meta_ref,
    query_ref,
    keys_ref,
    own_ref,
    other_ref,
    near_top,
    near_bottom,
    near_summed,
    out_ref,
    top,
    bottom,
    summed,
):
    top[...] = near_top[...]
    bottom[...] = near_bottom[...]
    summed[...] = near_summed[...]
    visit(meta_ref, 1, query_ref, keys_ref, own_ref, other_ref, top, bottom, summed)
    seg_len = keys_ref.shape[3]
    scaled = summed[...] / bottom[...]
    result = jnp.zeros((1, seg_len), jnp.float32)
    for h in range(query_ref.shape[1] // seg_len):
        part = scaled[:, h * seg_len : (h + 1) * seg_len]
        result += part[h : h + 1] + part[2 + h : 3 + h]
    for i in range(out_ref.shape[0]):
        out_ref[i] = jnp.broadcast_to(result, out_ref.shape[1:])


def finish_kernel(meta_ref, parts_ref, resid_ref, out_ref, leaf_ref):
    total = resid_ref[...] + jnp.sum(parts_ref[...], axis=0)[:1]
    index = lax.broadcasted_iota(jnp.int32, total.shape, 1)
    length = meta_ref[2]
    values = jnp.where(index < length, total, 0.0)
    out_ref[...] = values
    leaf = jnp.sum(jnp.where(index == length - 1, values, 0.0), axis=1, keepdims=True)
    leaf_ref[...] = jnp.broadcast_to(leaf, leaf_ref.shape)


def gathered(value, axis):
    return lax.all_to_all(value, axis, 0, 0)


def on_device(
    tokens, w_query, key_weight, value_weight, resid_head, head_readout, parents, placed, lengths
):
    seg_len, model_width = tokens.shape
    segments = parents.shape[0]
    fsdp_size = lax.axis_size(FSDP)
    quarters = lax.axis_size("x")
    pairs = segments // 2
    width = key_weight.shape[1]
    rows = width + 8
    heads = w_query.shape[1] // HEAD_SIZE
    swap = [(0, 1), (1, 0)]
    params = pltpu.CompilerParams(vmem_limit_bytes=VMEM_LIMIT)

    other = lax.ppermute(w_query, "zl", swap)
    values_x = gathered(jnp.broadcast_to(value_weight.T[None], (quarters, width, seg_len)), "x")
    readout = head_readout.reshape(heads, HEAD_SIZE).astype(jnp.float32)
    own_readout = lax.dynamic_slice(
        resid_head, (lax.axis_index(SEG) * seg_len,), (seg_len,)
    )
    key_rows = jnp.concatenate(
        [
            jnp.pad(key_weight.T.astype(jnp.float32), ((0, 4), (0, 0))),
            jnp.pad(own_readout.astype(jnp.float32)[None], ((0, 3), (0, 0))),
        ]
    )
    both = jnp.pad(w_query, ((0, w_query.shape[0]), (0, 0)))
    values_x, other, readout, key_rows, both = lax.optimization_barrier(
        (values_x, other, readout, key_rows, both)
    )
    both = lax.dynamic_update_slice(both, other, (w_query.shape[0], 0))
    query_weight = lax.all_gather(both, ("y", "c"), axis=0, tiled=True)
    pieces = pl.pallas_call(
        weights_kernel,
        out_shape=jax.ShapeDtypeStruct((pairs, rows, seg_len), jnp.bfloat16),
        in_specs=[VMEM_SPEC] * 3,
        out_specs=VMEM_SPEC,
        compiler_params=params,
        name="fold_weights",
    )(values_x, readout, key_rows)

    near_weights = gathered(pieces, ("y", "zl"))
    meta, table, positions = pl.pallas_call(
        tree_kernel,
        out_shape=(
            jax.ShapeDtypeStruct((META,), jnp.int32),
            jax.ShapeDtypeStruct((segments, 128), jnp.float32),
            jax.ShapeDtypeStruct((1, seg_len), jnp.float32),
        ),
        in_specs=[HBM_SPEC] * 3,
        out_specs=(SMEM_SPEC, VMEM_SPEC, VMEM_SPEC),
        scratch_shapes=[pltpu.SMEM((segments,), jnp.int32)] * 4
        + [pltpu.SemaphoreType.DMA((3,))],
        compiler_params=params,
        name="tree",
    )(parents, placed, lengths)
    dims = jnp.arange(HEAD_SIZE, dtype=jnp.int32)
    frequency = ROPE_BASE ** (-2.0 * (dims // 2).astype(jnp.float32) / HEAD_SIZE)
    angles = frequency[:, None] * positions
    cosine = jnp.cos(angles)
    sine = jnp.sin(angles) * jnp.where(dims % 2 == 0, -1.0, 1.0)[:, None]
    near_weights, cosine, sine = lax.optimization_barrier((near_weights, cosine, sine))

    far_weights = lax.ppermute(near_weights, "c", swap)
    near_sums = pl.pallas_call(
        near_keys_kernel,
        out_shape=jax.ShapeDtypeStruct((rows, seg_len), jnp.float32),
        in_specs=[VMEM_SPEC] * 2,
        out_specs=VMEM_SPEC,
        compiler_params=params,
        cost_estimate=pl.CostEstimate(
            flops=rows * seg_len * model_width, bytes_accessed=2**21, transcendentals=0
        ),
        name="project_near_keys",
    )(tokens, near_weights)
    far_weights, near_sums = lax.optimization_barrier((far_weights, near_sums))
    keys, residual = pl.pallas_call(
        far_keys_kernel,
        out_shape=(
            jax.ShapeDtypeStruct((lax.axis_size("y"), rows, seg_len), jnp.bfloat16),
            jax.ShapeDtypeStruct((1, seg_len), jnp.float32),
        ),
        in_specs=[VMEM_SPEC] * 5,
        out_specs=(VMEM_SPEC, VMEM_SPEC),
        scratch_shapes=[pltpu.VMEM((rows, seg_len), jnp.float32)],
        compiler_params=params,
        name="project_far_keys",
    )(tokens, far_weights, near_sums, cosine, sine)

    keys_y = gathered(keys, "y")
    spread = lax.axis_size(("zl", "x"))
    values = keys_y[:, width:]
    keys_y = keys_y[:, :width]
    near = gathered(jnp.broadcast_to(keys_y[None], (spread, *keys_y.shape)), ("zl", "x"))
    values = jnp.stack([values, lax.ppermute(values, "c", swap)])
    values, query_sine = lax.optimization_barrier((values, sine))
    other_values = lax.ppermute(values, "zl", swap)
    queries = pl.pallas_call(
        queries_kernel,
        out_shape=jax.ShapeDtypeStruct((HEAD_SIZE, heads * seg_len), jnp.bfloat16),
        in_specs=[VMEM_SPEC] * 4,
        out_specs=VMEM_SPEC,
        scratch_shapes=[pltpu.VMEM((seg_len, heads * HEAD_SIZE), jnp.float32)],
        cost_estimate=pl.CostEstimate(
            flops=2 * seg_len * model_width * heads * HEAD_SIZE,
            bytes_accessed=2 * model_width * (seg_len + heads * HEAD_SIZE),
            transcendentals=0,
        ),
        compiler_params=params,
        name="project_queries",
    )(tokens, query_weight.reshape(segments, seg_len, -1), cosine, query_sine)
    near, queries, other_values = lax.optimization_barrier((near, queries, other_values))
    far = lax.ppermute(near, "c", swap)
    columns = heads * seg_len
    state = (
        jax.ShapeDtypeStruct((1, columns), jnp.float32),
        jax.ShapeDtypeStruct((1, columns), jnp.float32),
        jax.ShapeDtypeStruct((8, columns), jnp.float32),
    )
    near_state = pl.pallas_call(
        near_kernel,
        out_shape=state,
        in_specs=[SMEM_SPEC] + [VMEM_SPEC] * 4,
        out_specs=(VMEM_SPEC,) * 3,
        compiler_params=params,
        cost_estimate=pl.CostEstimate(
            flops=2**28, bytes_accessed=2**21, transcendentals=2**19
        ),
        name="attend_near",
    )(meta, queries, near, values, other_values)
    far, near_state = lax.optimization_barrier((far, near_state))
    mixed = pl.pallas_call(
        far_kernel,
        out_shape=jax.ShapeDtypeStruct((fsdp_size, 8, seg_len), jnp.float32),
        in_specs=[SMEM_SPEC] + [VMEM_SPEC] * 7,
        out_specs=VMEM_SPEC,
        scratch_shapes=[pltpu.VMEM(part.shape, part.dtype) for part in state],
        compiler_params=params,
        name="attend_far",
    )(meta, queries, far, values, other_values, *near_state)
    parts = gathered(mixed, FSDP)
    token_values, leaf_rows = pl.pallas_call(
        finish_kernel,
        out_shape=(
            jax.ShapeDtypeStruct((1, seg_len), jnp.float32),
            jax.ShapeDtypeStruct((segments, 128), jnp.float32),
        ),
        in_specs=[SMEM_SPEC, VMEM_SPEC, VMEM_SPEC],
        out_specs=(VMEM_SPEC, VMEM_SPEC),
        compiler_params=params,
        name="token_values",
    )(meta, parts, residual)
    leaves = gathered(leaf_rows, SEG)
    branch = jnp.sum(leaves * table, axis=0)[:segments]
    return (token_values.reshape(seg_len), branch)


def solution(mesh):
    fine = Mesh(mesh.devices.reshape(8, 2, 2, 4, 4), SEG + FSDP)
    in_specs = (
        P(SEG, None),
        P(SEG, FSDP),
        P(SEG, FSDP),
        P(SEG, FSDP),
        P(),
        P(FSDP),
        P(),
        P(),
        P(),
    )
    out_specs = (P(SEG), P())
    return jax.shard_map(
        on_device, mesh=fine, in_specs=in_specs, out_specs=out_specs, check_vma=False
    )
```

```python
import jax
import jax.numpy as jnp
from jax import lax
from jax.experimental import pallas as pl
from jax.experimental.pallas import tpu as pltpu
from jax.sharding import Mesh
from jax.sharding import PartitionSpec as P

KEY_VALUE_HEADS = 4
HEAD_SIZE = 128
ROPE_BASE = 1000000.0
SEG = ("y", "zl", "c")
FSDP = ("zh", "x")
NEAR, FAR, LENGTHS, META = 8, 48, 80, 168
VMEM_LIMIT = 40 * 1024 * 1024

VMEM_SPEC = pl.BlockSpec(memory_space=pltpu.VMEM)
SMEM_SPEC = pl.BlockSpec(memory_space=pltpu.SMEM)
HBM_SPEC = pl.BlockSpec(memory_space=pltpu.HBM)


def tree_kernel(
    parents_src,
    placed_src,
    lengths_src,
    meta_ref,
    table_ref,
    position_ref,
    live_ref,
    last_ref,
    parents_ref,
    placed_ref,
    lengths_ref,
    slot_of,
    sems,
):
    copies = [
        pltpu.make_async_copy(source, there, sems.at[i])
        for i, (source, there) in enumerate(
            ((parents_src, parents_ref), (placed_src, placed_ref), (lengths_src, lengths_ref))
        )
    ]
    for copy in copies:
        copy.start()
    for copy in copies:
        copy.wait()
    segments = parents_ref.shape[0]
    slot = lax.axis_index(SEG)
    own = placed_ref[slot]

    def place(j, carry):
        slot_of[placed_ref[j]] = j
        return carry

    lax.fori_loop(0, segments, place, 0)

    def clear(j, carry):
        meta_ref[j] = 0
        return carry

    lax.fori_loop(0, META, clear, 0)

    def above(state):
        seg, near, far, offset = state
        there = slot_of[seg]
        is_near = (there % 2 == slot % 2).astype(jnp.int32)
        entry = jnp.where(is_near == 1, NEAR + near, FAR + far)
        meta_ref[entry] = there
        meta_ref[LENGTHS + entry] = lengths_ref[seg]
        return parents_ref[seg], near + is_near, far + 1 - is_near, offset + lengths_ref[seg]

    zero = jnp.int32(0)
    _, near, far, offset = lax.while_loop(
        lambda state: state[0] >= 0, above, (parents_ref[own], zero, zero, zero)
    )
    meta_ref[0] = near
    meta_ref[1] = far
    index = lax.broadcasted_iota(jnp.int32, position_ref.shape, 1)
    position_ref[...] = (offset + index).astype(jnp.float32)
    live_ref[...] = jnp.where(index < lengths_ref[own], 1.0, 0.0)
    last_ref[...] = jnp.where(index == lengths_ref[own] - 1, 1.0, 0.0)

    row = lax.broadcasted_iota(jnp.int32, (128, 128), 0)
    col = lax.broadcasted_iota(jnp.int32, (128, 128), 1)
    row_s = lax.broadcasted_iota(jnp.int32, (segments, 128), 0)
    col_s = lax.broadcasted_iota(jnp.int32, (segments, 128), 1)
    parent_of = jnp.full((segments, 128), -1, jnp.int32)
    held = jnp.full((segments, 128), -1, jnp.int32)
    for i in range(segments):
        parent_of = jnp.where(row_s == i, parents_ref[i], parent_of)
        held = jnp.where(row_s == i, placed_ref[i], held)
    step = jnp.where(parent_of == col_s, 1.0, 0.0)
    step = jnp.concatenate([step, jnp.zeros((128 - segments, 128), jnp.float32)], axis=0)
    ancestry = jnp.where(row == col, 1.0, 0.0) + step

    def times(a, b):
        return jnp.dot(
            a.astype(jnp.bfloat16), b.astype(jnp.bfloat16), preferred_element_type=jnp.float32
        )

    power = step
    reach = 1
    while 2 * reach <= segments:
        power = times(power, power)
        ancestry = ancestry + times(power, ancestry)
        reach *= 2
    children = jnp.sum(step, axis=0, keepdims=True)
    leafy = jnp.where((children < 0.5) & (col[:1] < segments), 1.0, 0.0)
    leaves = times(jnp.broadcast_to(leafy, (8, 128)), ancestry)[:1]
    placement = jnp.where(held == col_s, 1.0, 0.0)
    share = times(placement * leafy, ancestry)
    table_ref[...] = jnp.where(col_s < segments, share / jnp.maximum(leaves, 1.0), 0.0)


def weights_kernel(value_ref, readout_ref, key_ref, out_ref):
    quarters, part, rows = value_ref.shape
    value = value_ref[...].reshape(quarters * part, rows)
    readout = readout_ref[...].astype(jnp.bfloat16)
    folded = jnp.dot(readout, value, preferred_element_type=jnp.float32)
    high = folded.astype(jnp.bfloat16).astype(jnp.float32)
    low = folded - high
    width = key_ref.shape[0] - 8
    piece = jnp.concatenate([key_ref[:width], high, low, key_ref[width + 4 :]], axis=0)
    piece = piece.astype(jnp.bfloat16)
    for i in range(out_ref.shape[0]):
        out_ref[i] = piece


def turned(raw, cosine, sine, axis):
    extent = raw.shape[axis]
    index = lax.broadcasted_iota(jnp.int32, raw.shape, axis)
    after = pltpu.roll(raw, extent - 1, axis)
    before = pltpu.roll(raw, 1, axis)
    return raw * cosine + jnp.where(index % 2 == 0, after, before) * sine


def half_projected(tokens_ref, weights_ref, total, parity):
    for even in range(2):

        @pl.when(parity == even)
        def _():
            blocks, _, depth = weights_ref.shape
            acc = total[...]
            for p in range(blocks):
                start = (2 * p + even) * depth
                acc += lax.dot_general(
                    weights_ref[p],
                    tokens_ref[:, start : start + depth],
                    (((1,), (1,)), ((), ())),
                    preferred_element_type=jnp.float32,
                )
            total[...] = acc


def near_keys_kernel(tokens_ref, weights_ref, out_ref):
    out_ref[...] = jnp.zeros_like(out_ref)
    half_projected(tokens_ref, weights_ref, out_ref, lax.axis_index("c"))


def far_keys_kernel(
    tokens_ref, weights_ref, near_ref, cosine_ref, sine_ref, out_ref, resid_ref, total
):
    total[...] = near_ref[...]
    half_projected(tokens_ref, weights_ref, total, 1 - lax.axis_index("c"))
    width = total.shape[0] - 8
    start = pl.multiple_of(lax.axis_index("x") * width, width)
    keys = turned(total[:width], cosine_ref[pl.ds(start, width)], sine_ref[pl.ds(start, width)], 0)
    last = total[width:]
    row = lax.broadcasted_iota(jnp.int32, last.shape, 0)
    summed = last + pltpu.roll(last, 6, 0)
    high = summed.astype(jnp.bfloat16).astype(jnp.float32)
    low = pltpu.roll(summed - high, 2, 0)
    tail = jnp.where(row < 2, high, jnp.where(row < 4, low, 0.0))
    resid_ref[...] = last[4:5]
    piece = jnp.concatenate([keys, tail], axis=0).astype(jnp.bfloat16)
    for i in range(out_ref.shape[0]):
        out_ref[i] = piece


def queries_kernel(tokens_ref, weights_ref, cosine_ref, sine_ref, out_ref, total):
    blocks, depth, _ = weights_ref.shape
    seg_len = tokens_ref.shape[0]
    half = lax.axis_index("zl")
    for upper in range(2):

        @pl.when(half == upper)
        def _():
            acc = jnp.zeros_like(total)
            for i in range(blocks):
                block = i // 4 * 4 + (i % 2 ^ upper) * 2 + i // 2 % 2
                acc += jnp.dot(
                    tokens_ref[:, block * depth : (block + 1) * depth],
                    weights_ref[i],
                    preferred_element_type=jnp.float32,
                )
            total[...] = acc

    raw = total[...].T
    for h in range(raw.shape[0] // HEAD_SIZE):
        head = raw[h * HEAD_SIZE : (h + 1) * HEAD_SIZE]
        out_ref[:, h * seg_len : (h + 1) * seg_len] = turned(
            head, cosine_ref[...], sine_ref[...], 0
        ).astype(jnp.bfloat16)


def scored(query_ref, keys_ref, slot, seen):
    quarters = lax.axis_size("x")
    seg_len = keys_ref.shape[3]
    keys = keys_ref[pl.ds(slot // 2 % 2 * quarters, quarters), slot // 4]
    raw = lax.dot_general(
        keys.reshape(HEAD_SIZE, seg_len),
        query_ref[...],
        (((0,), (0,)), ((), ())),
        preferred_element_type=jnp.float32,
    )
    return jnp.where(seen, raw * HEAD_SIZE ** (-0.5), -1e30)


def mixed_values(own_ref, other_ref, far, slot, weights):
    is_other = slot // 2 % 2 != lax.axis_index("zl")
    own, other = (ref[far, slot // 4].astype(jnp.float32) for ref in (own_ref, other_ref))
    return jnp.dot(
        jnp.where(is_other, other, own).astype(jnp.bfloat16),
        weights.astype(jnp.bfloat16),
        preferred_element_type=jnp.float32,
    )


def visit(meta_ref, far, query_ref, keys_ref, own_ref, other_ref, top, bottom, summed):
    key_at = lax.broadcasted_iota(jnp.int32, (keys_ref.shape[3], query_ref.shape[1]), 0)
    first = (NEAR, FAR)[far]

    def two(n, carry):
        entries = [first + 2 * n, first + 2 * n + 1]
        slots = [meta_ref[e] for e in entries]
        masked = [
            scored(query_ref, keys_ref, slot, key_at < meta_ref[LENGTHS + e])
            for e, slot in zip(entries, slots)
        ]
        peak = jnp.max(jnp.maximum(masked[0], masked[1]), axis=0, keepdims=True)
        peak = jnp.maximum(top[...], peak)
        shrink = jnp.exp(top[...] - peak)
        weights = [jnp.exp(m - peak) for m in masked]
        top[...] = peak
        bottom[...] = bottom[...] * shrink + jnp.sum(
            weights[0] + weights[1], axis=0, keepdims=True
        )
        summed[...] = (
            summed[...] * shrink
            + mixed_values(own_ref, other_ref, far, slots[0], weights[0])
            + mixed_values(own_ref, other_ref, far, slots[1], weights[1])
        )
        return carry

    lax.fori_loop(0, (meta_ref[far] + 1) // 2, two, 0)


def near_kernel(meta_ref, query_ref, keys_ref, own_ref, other_ref, top, bottom, summed):
    seg_len = keys_ref.shape[3]
    shape = (seg_len, query_ref.shape[1])
    key_at = lax.broadcasted_iota(jnp.int32, shape, 0)
    query_at = lax.broadcasted_iota(jnp.int32, shape, 1) % seg_len
    own = lax.axis_index(SEG)
    masked = scored(query_ref, keys_ref, own, key_at <= query_at)
    peak = jnp.max(masked, axis=0, keepdims=True)
    weights = jnp.exp(masked - peak)
    top[...] = peak
    bottom[...] = jnp.sum(weights, axis=0, keepdims=True)
    summed[...] = mixed_values(own_ref, other_ref, 0, own, weights)
    visit(meta_ref, 0, query_ref, keys_ref, own_ref, other_ref, top, bottom, summed)


def far_kernel(
    meta_ref,
    query_ref,
    keys_ref,
    own_ref,
    other_ref,
    near_top,
    near_bottom,
    near_summed,
    out_ref,
    top,
    bottom,
    summed,
):
    top[...] = near_top[...]
    bottom[...] = near_bottom[...]
    summed[...] = near_summed[...]
    visit(meta_ref, 1, query_ref, keys_ref, own_ref, other_ref, top, bottom, summed)
    seg_len = keys_ref.shape[3]
    scaled = summed[...] / bottom[...]
    result = jnp.zeros((1, seg_len), jnp.float32)
    for h in range(query_ref.shape[1] // seg_len):
        part = scaled[:, h * seg_len : (h + 1) * seg_len]
        result += part[h : h + 1] + part[2 + h : 3 + h]
    for i in range(out_ref.shape[0]):
        out_ref[i] = jnp.broadcast_to(result, out_ref.shape[1:])


def finish_kernel(parts_ref, resid_ref, live_ref, last_ref, out_ref, leaf_ref):
    total = resid_ref[...] + jnp.sum(parts_ref[...], axis=0)[:1]
    values = jnp.where(live_ref[...] > 0.5, total, 0.0)
    out_ref[...] = values
    leaf = jnp.sum(jnp.where(last_ref[...] > 0.5, values, 0.0), axis=1, keepdims=True)
    leaf_ref[...] = jnp.broadcast_to(leaf, leaf_ref.shape)


def gathered(value, axis):
    return lax.all_to_all(value, axis, 0, 0)


def on_device(
    tokens, w_query, key_weight, value_weight, resid_head, head_readout, parents, placed, lengths
):
    seg_len, model_width = tokens.shape
    segments = parents.shape[0]
    fsdp_size = lax.axis_size(FSDP)
    quarters = lax.axis_size("x")
    pairs = segments // 2
    width = key_weight.shape[1]
    rows = width + 8
    heads = w_query.shape[1] // HEAD_SIZE
    swap = [(0, 1), (1, 0)]
    params = pltpu.CompilerParams(vmem_limit_bytes=VMEM_LIMIT)

    sent = jnp.broadcast_to(value_weight.T[None], (quarters, width, seg_len))
    sent, w_query = lax.optimization_barrier((sent, w_query))
    other = lax.ppermute(w_query, "zl", swap)
    values_x = gathered(sent, "x")
    readout = head_readout.reshape(heads, HEAD_SIZE).astype(jnp.float32)
    own_readout = lax.dynamic_slice(
        resid_head, (lax.axis_index(SEG) * seg_len,), (seg_len,)
    )
    key_rows = jnp.concatenate(
        [
            jnp.pad(key_weight.T.astype(jnp.float32), ((0, 4), (0, 0))),
            jnp.pad(own_readout.astype(jnp.float32)[None], ((0, 3), (0, 0))),
        ]
    )
    both = jnp.pad(w_query, ((0, w_query.shape[0]), (0, 0)))
    values_x, other, readout, key_rows, both = lax.optimization_barrier(
        (values_x, other, readout, key_rows, both)
    )
    both = lax.dynamic_update_slice(both, other, (w_query.shape[0], 0))
    query_weight = lax.all_gather(both, ("y", "c"), axis=0, tiled=True)
    pieces = pl.pallas_call(
        weights_kernel,
        out_shape=jax.ShapeDtypeStruct((pairs, rows, seg_len), jnp.bfloat16),
        in_specs=[VMEM_SPEC] * 3,
        out_specs=VMEM_SPEC,
        compiler_params=params,
        name="fold_weights",
    )(values_x, readout, key_rows)

    near_weights = gathered(pieces, ("y", "zl"))
    by_token = jax.ShapeDtypeStruct((1, seg_len), jnp.float32)
    meta, table, positions, live, last = pl.pallas_call(
        tree_kernel,
        out_shape=(
            jax.ShapeDtypeStruct((META,), jnp.int32),
            jax.ShapeDtypeStruct((segments, 128), jnp.float32),
            by_token,
            by_token,
            by_token,
        ),
        in_specs=[HBM_SPEC] * 3,
        out_specs=(SMEM_SPEC,) + (VMEM_SPEC,) * 4,
        scratch_shapes=[pltpu.SMEM((segments,), jnp.int32)] * 4
        + [pltpu.SemaphoreType.DMA((3,))],
        compiler_params=params,
        name="tree",
    )(parents, placed, lengths)
    dims = jnp.arange(HEAD_SIZE, dtype=jnp.int32)
    frequency = ROPE_BASE ** (-2.0 * (dims // 2).astype(jnp.float32) / HEAD_SIZE)
    angles = frequency[:, None] * positions
    cosine = jnp.cos(angles)
    sine = jnp.sin(angles) * jnp.where(dims % 2 == 0, -1.0, 1.0)[:, None]
    near_weights, cosine, sine = lax.optimization_barrier((near_weights, cosine, sine))

    far_weights = lax.ppermute(near_weights, "c", swap)
    near_sums = pl.pallas_call(
        near_keys_kernel,
        out_shape=jax.ShapeDtypeStruct((rows, seg_len), jnp.float32),
        in_specs=[VMEM_SPEC] * 2,
        out_specs=VMEM_SPEC,
        compiler_params=params,
        cost_estimate=pl.CostEstimate(
            flops=rows * seg_len * model_width, bytes_accessed=2**21, transcendentals=0
        ),
        name="project_near_keys",
    )(tokens, near_weights)
    far_weights, near_sums = lax.optimization_barrier((far_weights, near_sums))
    keys, residual = pl.pallas_call(
        far_keys_kernel,
        out_shape=(
            jax.ShapeDtypeStruct((lax.axis_size("y"), rows, seg_len), jnp.bfloat16),
            jax.ShapeDtypeStruct((1, seg_len), jnp.float32),
        ),
        in_specs=[VMEM_SPEC] * 5,
        out_specs=(VMEM_SPEC, VMEM_SPEC),
        scratch_shapes=[pltpu.VMEM((rows, seg_len), jnp.float32)],
        compiler_params=params,
        name="project_far_keys",
    )(tokens, far_weights, near_sums, cosine, sine)

    keys_y = gathered(keys, "y")
    spread = lax.axis_size(("zl", "x"))
    values = keys_y[:, width:]
    keys_y = keys_y[:, :width]
    near = gathered(jnp.broadcast_to(keys_y[None], (spread, *keys_y.shape)), ("zl", "x"))
    values = jnp.stack([values, lax.ppermute(values, "c", swap)])
    values, query_sine = lax.optimization_barrier((values, sine))
    other_values = lax.ppermute(values, "zl", swap)
    queries = pl.pallas_call(
        queries_kernel,
        out_shape=jax.ShapeDtypeStruct((HEAD_SIZE, heads * seg_len), jnp.bfloat16),
        in_specs=[VMEM_SPEC] * 4,
        out_specs=VMEM_SPEC,
        scratch_shapes=[pltpu.VMEM((seg_len, heads * HEAD_SIZE), jnp.float32)],
        cost_estimate=pl.CostEstimate(
            flops=2 * seg_len * model_width * heads * HEAD_SIZE,
            bytes_accessed=2 * model_width * (seg_len + heads * HEAD_SIZE),
            transcendentals=0,
        ),
        compiler_params=params,
        name="project_queries",
    )(tokens, query_weight.reshape(segments, seg_len, -1), cosine, query_sine)
    near, queries, other_values = lax.optimization_barrier((near, queries, other_values))
    far = lax.ppermute(near, "c", swap)
    columns = heads * seg_len
    state = (
        jax.ShapeDtypeStruct((1, columns), jnp.float32),
        jax.ShapeDtypeStruct((1, columns), jnp.float32),
        jax.ShapeDtypeStruct((8, columns), jnp.float32),
    )
    near_state = pl.pallas_call(
        near_kernel,
        out_shape=state,
        in_specs=[SMEM_SPEC] + [VMEM_SPEC] * 4,
        out_specs=(VMEM_SPEC,) * 3,
        compiler_params=params,
        cost_estimate=pl.CostEstimate(
            flops=2**28, bytes_accessed=2**21, transcendentals=2**19
        ),
        name="attend_near",
    )(meta, queries, near, values, other_values)
    far, near_state = lax.optimization_barrier((far, near_state))
    mixed = pl.pallas_call(
        far_kernel,
        out_shape=jax.ShapeDtypeStruct((fsdp_size, 8, seg_len), jnp.float32),
        in_specs=[SMEM_SPEC] + [VMEM_SPEC] * 7,
        out_specs=VMEM_SPEC,
        scratch_shapes=[pltpu.VMEM(part.shape, part.dtype) for part in state],
        compiler_params=params,
        name="attend_far",
    )(meta, queries, far, values, other_values, *near_state)
    parts = gathered(mixed, FSDP)
    token_values, leaf_rows = pl.pallas_call(
        finish_kernel,
        out_shape=(
            jax.ShapeDtypeStruct((1, seg_len), jnp.float32),
            jax.ShapeDtypeStruct((segments, 128), jnp.float32),
        ),
        in_specs=[VMEM_SPEC] * 4,
        out_specs=(VMEM_SPEC, VMEM_SPEC),
        compiler_params=params,
        name="token_values",
    )(parts, residual, live, last)
    leaves = gathered(leaf_rows, SEG)
    branch = jnp.sum(leaves * table, axis=0)[:segments]
    return (token_values.reshape(seg_len), branch)


def solution(mesh):
    fine = Mesh(mesh.devices.reshape(8, 2, 2, 4, 4), SEG + FSDP)
    in_specs = (
        P(SEG, None),
        P(SEG, FSDP),
        P(SEG, FSDP),
        P(SEG, FSDP),
        P(),
        P(FSDP),
        P(),
        P(),
        P(),
    )
    out_specs = (P(SEG), P())
    return jax.shard_map(
        on_device, mesh=fine, in_specs=in_specs, out_specs=out_specs, check_vma=False
    )
```

```python
import jax
import jax.numpy as jnp
from jax import lax
from jax.experimental import pallas as pl
from jax.experimental.pallas import tpu as pltpu
from jax.sharding import Mesh
from jax.sharding import PartitionSpec as P

KEY_VALUE_HEADS = 4
HEAD_SIZE = 128
ROPE_BASE = 1000000.0
SEG = ("y", "zl", "c")
FSDP = ("zh", "x")
NEAR, FAR, LENGTHS, META = 8, 48, 80, 168
UNSEEN = -1e30
LOG2_E = 1.4426950408889634
VMEM_LIMIT = 40 * 1024 * 1024

VMEM_SPEC = pl.BlockSpec(memory_space=pltpu.VMEM)
SMEM_SPEC = pl.BlockSpec(memory_space=pltpu.SMEM)
HBM_SPEC = pl.BlockSpec(memory_space=pltpu.HBM)


def tree_kernel(
    parents_src,
    placed_src,
    lengths_src,
    meta_ref,
    table_ref,
    position_ref,
    live_ref,
    last_ref,
    parents_ref,
    placed_ref,
    lengths_ref,
    slot_of,
    sems,
):
    copies = [
        pltpu.make_async_copy(source, there, sems.at[i])
        for i, (source, there) in enumerate(
            ((parents_src, parents_ref), (placed_src, placed_ref), (lengths_src, lengths_ref))
        )
    ]
    for copy in copies:
        copy.start()
    for copy in copies:
        copy.wait()
    segments = parents_ref.shape[0]
    slot = lax.axis_index(SEG)
    own = placed_ref[slot]

    def place(j, carry):
        slot_of[placed_ref[j]] = j
        return carry

    lax.fori_loop(0, segments, place, 0)

    def clear(j, carry):
        meta_ref[j] = 0
        return carry

    lax.fori_loop(0, META, clear, 0)

    def above(state):
        seg, near, far, offset = state
        there = slot_of[seg]
        is_near = (there % 2 == slot % 2).astype(jnp.int32)
        entry = jnp.where(is_near == 1, NEAR + near, FAR + far)
        meta_ref[entry] = there
        meta_ref[LENGTHS + entry] = lengths_ref[seg]
        return parents_ref[seg], near + is_near, far + 1 - is_near, offset + lengths_ref[seg]

    zero = jnp.int32(0)
    _, near, far, offset = lax.while_loop(
        lambda state: state[0] >= 0, above, (parents_ref[own], zero, zero, zero)
    )
    meta_ref[0] = near
    meta_ref[1] = far
    index = lax.broadcasted_iota(jnp.int32, position_ref.shape, 1)
    position_ref[...] = (offset + index).astype(jnp.float32)
    live_ref[...] = jnp.where(index < lengths_ref[own], 1.0, 0.0)
    last_ref[...] = jnp.where(index == lengths_ref[own] - 1, 1.0, 0.0)

    row = lax.broadcasted_iota(jnp.int32, (128, 128), 0)
    col = lax.broadcasted_iota(jnp.int32, (128, 128), 1)
    row_s = lax.broadcasted_iota(jnp.int32, (segments, 128), 0)
    col_s = lax.broadcasted_iota(jnp.int32, (segments, 128), 1)
    parent_of = jnp.full((segments, 128), -1, jnp.int32)
    held = jnp.full((segments, 128), -1, jnp.int32)
    for i in range(segments):
        parent_of = jnp.where(row_s == i, parents_ref[i], parent_of)
        held = jnp.where(row_s == i, placed_ref[i], held)
    step = jnp.where(parent_of == col_s, 1.0, 0.0)
    step = jnp.concatenate([step, jnp.zeros((128 - segments, 128), jnp.float32)], axis=0)
    ancestry = jnp.where(row == col, 1.0, 0.0) + step

    def times(a, b):
        return jnp.dot(
            a.astype(jnp.bfloat16), b.astype(jnp.bfloat16), preferred_element_type=jnp.float32
        )

    power = step
    reach = 1
    while 2 * reach <= segments:
        power = times(power, power)
        ancestry = ancestry + times(power, ancestry)
        reach *= 2
    children = jnp.sum(step, axis=0, keepdims=True)
    leafy = jnp.where((children < 0.5) & (col[:1] < segments), 1.0, 0.0)
    leaves = times(jnp.broadcast_to(leafy, (8, 128)), ancestry)[:1]
    placement = jnp.where(held == col_s, 1.0, 0.0)
    share = times(placement * leafy, ancestry)
    table_ref[...] = jnp.where(col_s < segments, share / jnp.maximum(leaves, 1.0), 0.0)


def weights_kernel(value_ref, readout_ref, key_ref, out_ref):
    quarters, part, rows = value_ref.shape
    value = value_ref[...].reshape(quarters * part, rows)
    readout = readout_ref[...].astype(jnp.bfloat16)
    folded = jnp.dot(readout, value, preferred_element_type=jnp.float32)
    high = folded.astype(jnp.bfloat16).astype(jnp.float32)
    low = folded - high
    width = key_ref.shape[0] - 8
    piece = jnp.concatenate([key_ref[:width], high, low, key_ref[width + 4 :]], axis=0)
    piece = piece.astype(jnp.bfloat16)
    for i in range(out_ref.shape[0]):
        out_ref[i] = piece


def turned(raw, cosine, sine, axis):
    extent = raw.shape[axis]
    index = lax.broadcasted_iota(jnp.int32, raw.shape, axis)
    after = pltpu.roll(raw, extent - 1, axis)
    before = pltpu.roll(raw, 1, axis)
    return raw * cosine + jnp.where(index % 2 == 0, after, before) * sine


def half_projected(tokens_ref, weights_ref, total, parity):
    for even in range(2):

        @pl.when(parity == even)
        def _():
            blocks, _, depth = weights_ref.shape
            acc = total[...]
            for p in range(blocks):
                start = (2 * p + even) * depth
                acc += lax.dot_general(
                    weights_ref[p],
                    tokens_ref[:, start : start + depth],
                    (((1,), (1,)), ((), ())),
                    preferred_element_type=jnp.float32,
                )
            total[...] = acc


def near_keys_kernel(tokens_ref, weights_ref, out_ref):
    out_ref[...] = jnp.zeros_like(out_ref)
    half_projected(tokens_ref, weights_ref, out_ref, lax.axis_index("c"))


def far_keys_kernel(
    tokens_ref, weights_ref, near_ref, cosine_ref, sine_ref, out_ref, resid_ref, total
):
    total[...] = near_ref[...]
    half_projected(tokens_ref, weights_ref, total, 1 - lax.axis_index("c"))
    width = total.shape[0] - 8
    start = pl.multiple_of(lax.axis_index("x") * width, width)
    keys = turned(total[:width], cosine_ref[pl.ds(start, width)], sine_ref[pl.ds(start, width)], 0)
    last = total[width:]
    row = lax.broadcasted_iota(jnp.int32, last.shape, 0)
    summed = last + pltpu.roll(last, 6, 0)
    high = summed.astype(jnp.bfloat16).astype(jnp.float32)
    low = pltpu.roll(summed - high, 2, 0)
    tail = jnp.where(row < 2, high, jnp.where(row < 4, low, 0.0))
    resid_ref[...] = last[4:5]
    piece = jnp.concatenate([keys, tail], axis=0).astype(jnp.bfloat16)
    for i in range(out_ref.shape[0]):
        out_ref[i] = piece


def queries_kernel(tokens_ref, weights_ref, cosine_ref, sine_ref, out_ref, total):
    blocks, depth, _ = weights_ref.shape
    seg_len = tokens_ref.shape[0]
    half = lax.axis_index("zl")
    for upper in range(2):

        @pl.when(half == upper)
        def _():
            acc = jnp.zeros_like(total)
            for i in range(blocks):
                block = i // 4 * 4 + (i % 2 ^ upper) * 2 + i // 2 % 2
                acc += jnp.dot(
                    tokens_ref[:, block * depth : (block + 1) * depth],
                    weights_ref[i],
                    preferred_element_type=jnp.float32,
                )
            total[...] = acc

    raw = total[...].T
    for h in range(raw.shape[0] // HEAD_SIZE):
        head = raw[h * HEAD_SIZE : (h + 1) * HEAD_SIZE]
        out_ref[:, h * seg_len : (h + 1) * seg_len] = turned(
            head, cosine_ref[...], sine_ref[...], 0
        ).astype(jnp.bfloat16)


def spread_kernel(keys_ref, out_ref, sems):
    copies = [
        pltpu.make_async_copy(keys_ref, out_ref.at[i], sems.at[i]) for i in range(out_ref.shape[0])
    ]
    for copy in copies:
        copy.start()
    for copy in copies:
        copy.wait()


def scored(query_ref, keys_ref, slot):
    quarters = lax.axis_size("x")
    seg_len = keys_ref.shape[3]
    keys = keys_ref[pl.ds(slot // 2 % 2 * quarters, quarters), slot // 4]
    raw = lax.dot_general(
        keys.reshape(HEAD_SIZE, seg_len),
        query_ref[...],
        (((0,), (0,)), ((), ())),
        preferred_element_type=jnp.float32,
    )
    return raw * (HEAD_SIZE ** (-0.5) * LOG2_E)


def mixed_values(own_ref, other_ref, far, slot, weights):
    is_other = slot // 2 % 2 != lax.axis_index("zl")
    own, other = (ref[far, slot // 4].astype(jnp.float32) for ref in (own_ref, other_ref))
    return jnp.dot(
        jnp.where(is_other, other, own).astype(jnp.bfloat16),
        weights.astype(jnp.bfloat16),
        preferred_element_type=jnp.float32,
    )


def visit(meta_ref, far, query_ref, keys_ref, own_ref, other_ref, top, bottom, summed):
    key_at = lax.broadcasted_iota(jnp.int32, (keys_ref.shape[3], query_ref.shape[1]), 0)[:, :1]
    first = (NEAR, FAR)[far]

    def two(n, carry):
        entries = [first + 2 * n, first + 2 * n + 1]
        slots = [meta_ref[e] for e in entries]
        masked = [
            scored(query_ref, keys_ref, slot)
            + jnp.where(key_at < meta_ref[LENGTHS + e], 0.0, UNSEEN)
            for e, slot in zip(entries, slots)
        ]
        peak = jnp.max(jnp.maximum(masked[0], masked[1]), axis=0, keepdims=True)
        peak = jnp.maximum(top[...], peak)
        shrink = jnp.exp2(top[...] - peak)
        weights = [jnp.exp2(m - peak) for m in masked]
        top[...] = peak
        bottom[...] = bottom[...] * shrink + jnp.sum(
            weights[0] + weights[1], axis=0, keepdims=True
        )
        summed[...] = (
            summed[...] * shrink
            + mixed_values(own_ref, other_ref, far, slots[0], weights[0])
            + mixed_values(own_ref, other_ref, far, slots[1], weights[1])
        )
        return carry

    lax.fori_loop(0, (meta_ref[far] + 1) // 2, two, 0)


def near_kernel(meta_ref, query_ref, keys_ref, own_ref, other_ref, top, bottom, summed):
    seg_len = keys_ref.shape[3]
    shape = (seg_len, query_ref.shape[1])
    key_at = lax.broadcasted_iota(jnp.int32, shape, 0)
    query_at = lax.broadcasted_iota(jnp.int32, shape, 1) % seg_len
    own = lax.axis_index(SEG)
    masked = jnp.where(key_at <= query_at, scored(query_ref, keys_ref, own), UNSEEN)
    peak = jnp.max(masked, axis=0, keepdims=True)
    weights = jnp.exp2(masked - peak)
    top[...] = peak
    bottom[...] = jnp.sum(weights, axis=0, keepdims=True)
    summed[...] = mixed_values(own_ref, other_ref, 0, own, weights)
    visit(meta_ref, 0, query_ref, keys_ref, own_ref, other_ref, top, bottom, summed)


def far_kernel(
    meta_ref,
    query_ref,
    keys_ref,
    own_ref,
    other_ref,
    near_top,
    near_bottom,
    near_summed,
    out_ref,
    top,
    bottom,
    summed,
):
    top[...] = near_top[...]
    bottom[...] = near_bottom[...]
    summed[...] = near_summed[...]
    visit(meta_ref, 1, query_ref, keys_ref, own_ref, other_ref, top, bottom, summed)
    seg_len = keys_ref.shape[3]
    scaled = summed[...] / bottom[...]
    result = jnp.zeros((1, seg_len), jnp.float32)
    for h in range(query_ref.shape[1] // seg_len):
        part = scaled[:, h * seg_len : (h + 1) * seg_len]
        result += part[h : h + 1] + part[2 + h : 3 + h]
    for i in range(out_ref.shape[0]):
        out_ref[i] = result


def finish_kernel(parts_ref, resid_ref, live_ref, last_ref, out_ref, leaf_ref):
    total = resid_ref[...] + jnp.sum(parts_ref[...], axis=0)
    values = jnp.where(live_ref[...] > 0.5, total, 0.0)
    out_ref[...] = values
    leaf = jnp.sum(jnp.where(last_ref[...] > 0.5, values, 0.0), axis=1, keepdims=True)
    leaf_ref[...] = jnp.broadcast_to(leaf, leaf_ref.shape)


def gathered(value, axis):
    return lax.all_to_all(value, axis, 0, 0)


def on_device(
    tokens, w_query, key_weight, value_weight, resid_head, head_readout, parents, placed, lengths
):
    seg_len, model_width = tokens.shape
    segments = parents.shape[0]
    fsdp_size = lax.axis_size(FSDP)
    quarters = lax.axis_size("x")
    pairs = segments // 2
    width = key_weight.shape[1]
    rows = width + 8
    heads = w_query.shape[1] // HEAD_SIZE
    swap = [(0, 1), (1, 0)]
    params = pltpu.CompilerParams(vmem_limit_bytes=VMEM_LIMIT)

    sent = jnp.broadcast_to(value_weight.T[None], (quarters, width, seg_len))
    sent, w_query = lax.optimization_barrier((sent, w_query))
    other = lax.ppermute(w_query, "zl", swap)
    values_x = gathered(sent, "x")
    readout = head_readout.reshape(heads, HEAD_SIZE).astype(jnp.float32)
    own_readout = lax.dynamic_slice(
        resid_head, (lax.axis_index(SEG) * seg_len,), (seg_len,)
    )
    key_rows = jnp.concatenate(
        [
            jnp.pad(key_weight.T.astype(jnp.float32), ((0, 4), (0, 0))),
            jnp.pad(own_readout.astype(jnp.float32)[None], ((0, 3), (0, 0))),
        ]
    )
    both = jnp.pad(w_query, ((0, w_query.shape[0]), (0, 0)))
    values_x, other, readout, key_rows, both = lax.optimization_barrier(
        (values_x, other, readout, key_rows, both)
    )
    both = lax.dynamic_update_slice(both, other, (w_query.shape[0], 0))
    query_weight = lax.all_gather(both, ("y", "c"), axis=0, tiled=True)
    pieces = pl.pallas_call(
        weights_kernel,
        out_shape=jax.ShapeDtypeStruct((pairs, rows, seg_len), jnp.bfloat16),
        in_specs=[VMEM_SPEC] * 3,
        out_specs=VMEM_SPEC,
        compiler_params=params,
        name="fold_weights",
    )(values_x, readout, key_rows)

    near_weights = gathered(pieces, ("y", "zl"))
    by_token = jax.ShapeDtypeStruct((1, seg_len), jnp.float32)
    meta, table, positions, live, last = pl.pallas_call(
        tree_kernel,
        out_shape=(
            jax.ShapeDtypeStruct((META,), jnp.int32),
            jax.ShapeDtypeStruct((segments, 128), jnp.float32),
            by_token,
            by_token,
            by_token,
        ),
        in_specs=[HBM_SPEC] * 3,
        out_specs=(SMEM_SPEC,) + (VMEM_SPEC,) * 4,
        scratch_shapes=[pltpu.SMEM((segments,), jnp.int32)] * 4
        + [pltpu.SemaphoreType.DMA((3,))],
        compiler_params=params,
        name="tree",
    )(parents, placed, lengths)
    dims = jnp.arange(HEAD_SIZE, dtype=jnp.int32)
    frequency = ROPE_BASE ** (-2.0 * (dims // 2).astype(jnp.float32) / HEAD_SIZE)
    angles = frequency[:, None] * positions
    cosine = jnp.cos(angles)
    sine = jnp.sin(angles) * jnp.where(dims % 2 == 0, -1.0, 1.0)[:, None]
    near_weights, cosine, sine = lax.optimization_barrier((near_weights, cosine, sine))

    far_weights = lax.ppermute(near_weights, "c", swap)
    near_sums = pl.pallas_call(
        near_keys_kernel,
        out_shape=jax.ShapeDtypeStruct((rows, seg_len), jnp.float32),
        in_specs=[VMEM_SPEC] * 2,
        out_specs=VMEM_SPEC,
        compiler_params=params,
        cost_estimate=pl.CostEstimate(
            flops=rows * seg_len * model_width, bytes_accessed=2**21, transcendentals=0
        ),
        name="project_near_keys",
    )(tokens, near_weights)
    far_weights, near_sums = lax.optimization_barrier((far_weights, near_sums))
    keys, residual = pl.pallas_call(
        far_keys_kernel,
        out_shape=(
            jax.ShapeDtypeStruct((lax.axis_size("y"), rows, seg_len), jnp.bfloat16),
            jax.ShapeDtypeStruct((1, seg_len), jnp.float32),
        ),
        in_specs=[VMEM_SPEC] * 5,
        out_specs=(VMEM_SPEC, VMEM_SPEC),
        scratch_shapes=[pltpu.VMEM((rows, seg_len), jnp.float32)],
        compiler_params=params,
        name="project_far_keys",
    )(tokens, far_weights, near_sums, cosine, sine)

    keys_y = gathered(keys, "y")
    spread = lax.axis_size(("zl", "x"))
    values = keys_y[:, width:]
    keys_y = keys_y[:, :width]
    copies = pl.pallas_call(
        spread_kernel,
        out_shape=jax.ShapeDtypeStruct((spread, *keys_y.shape), keys_y.dtype),
        in_specs=[VMEM_SPEC],
        out_specs=HBM_SPEC,
        scratch_shapes=[pltpu.SemaphoreType.DMA((spread,))],
        compiler_params=params,
        name="spread_keys",
    )(keys_y)
    near = gathered(copies, ("zl", "x"))
    values = jnp.stack([values, lax.ppermute(values, "c", swap)])
    values, query_sine = lax.optimization_barrier((values, sine))
    other_values = lax.ppermute(values, "zl", swap)
    queries = pl.pallas_call(
        queries_kernel,
        out_shape=jax.ShapeDtypeStruct((HEAD_SIZE, heads * seg_len), jnp.bfloat16),
        in_specs=[VMEM_SPEC] * 4,
        out_specs=VMEM_SPEC,
        scratch_shapes=[pltpu.VMEM((seg_len, heads * HEAD_SIZE), jnp.float32)],
        cost_estimate=pl.CostEstimate(
            flops=2 * seg_len * model_width * heads * HEAD_SIZE,
            bytes_accessed=2 * model_width * (seg_len + heads * HEAD_SIZE),
            transcendentals=0,
        ),
        compiler_params=params,
        name="project_queries",
    )(tokens, query_weight.reshape(segments, seg_len, -1), cosine, query_sine)
    near, queries, other_values = lax.optimization_barrier((near, queries, other_values))
    far = lax.ppermute(near, "c", swap)
    columns = heads * seg_len
    state = (
        jax.ShapeDtypeStruct((1, columns), jnp.float32),
        jax.ShapeDtypeStruct((1, columns), jnp.float32),
        jax.ShapeDtypeStruct((8, columns), jnp.float32),
    )
    near_state = pl.pallas_call(
        near_kernel,
        out_shape=state,
        in_specs=[SMEM_SPEC] + [VMEM_SPEC] * 4,
        out_specs=(VMEM_SPEC,) * 3,
        compiler_params=params,
        cost_estimate=pl.CostEstimate(
            flops=2**28, bytes_accessed=2**21, transcendentals=2**19
        ),
        name="attend_near",
    )(meta, queries, near, values, other_values)
    far, near_state = lax.optimization_barrier((far, near_state))
    mixed = pl.pallas_call(
        far_kernel,
        out_shape=jax.ShapeDtypeStruct((fsdp_size, 1, seg_len), jnp.float32),
        in_specs=[SMEM_SPEC] + [VMEM_SPEC] * 7,
        out_specs=VMEM_SPEC,
        scratch_shapes=[pltpu.VMEM(part.shape, part.dtype) for part in state],
        compiler_params=params,
        name="attend_far",
    )(meta, queries, far, values, other_values, *near_state)
    parts = gathered(mixed, FSDP)
    token_values, leaf_rows = pl.pallas_call(
        finish_kernel,
        out_shape=(
            jax.ShapeDtypeStruct((1, seg_len), jnp.float32),
            jax.ShapeDtypeStruct((segments, 128), jnp.float32),
        ),
        in_specs=[VMEM_SPEC] * 4,
        out_specs=(VMEM_SPEC, VMEM_SPEC),
        compiler_params=params,
        name="token_values",
    )(parts, residual, live, last)
    leaves = gathered(leaf_rows, SEG)
    branch = jnp.sum(leaves * table, axis=0)[:segments]
    return (token_values.reshape(seg_len), branch)


def solution(mesh):
    fine = Mesh(mesh.devices.reshape(8, 2, 2, 4, 4), SEG + FSDP)
    in_specs = (
        P(SEG, None),
        P(SEG, FSDP),
        P(SEG, FSDP),
        P(SEG, FSDP),
        P(),
        P(FSDP),
        P(),
        P(),
        P(),
    )
    out_specs = (P(SEG), P())
    return jax.shard_map(
        on_device, mesh=fine, in_specs=in_specs, out_specs=out_specs, check_vma=False
    )
```

```python
import jax
import jax.numpy as jnp
from jax import lax
from jax.experimental import pallas as pl
from jax.experimental.pallas import tpu as pltpu
from jax.sharding import Mesh
from jax.sharding import PartitionSpec as P

KEY_VALUE_HEADS = 4
HEAD_SIZE = 128
ROPE_BASE = 1000000.0
SEG = ("y", "zl", "c")
FSDP = ("zh", "x")
NEAR, FAR, LENGTHS, META = 8, 48, 80, 168
UNSEEN = -1e30
LOG2_E = 1.4426950408889634
VMEM_LIMIT = 40 * 1024 * 1024

VMEM_SPEC = pl.BlockSpec(memory_space=pltpu.VMEM)
SMEM_SPEC = pl.BlockSpec(memory_space=pltpu.SMEM)
HBM_SPEC = pl.BlockSpec(memory_space=pltpu.HBM)


def tree_kernel(
    parents_src,
    placed_src,
    lengths_src,
    meta_ref,
    table_ref,
    position_ref,
    span_ref,
    parents_ref,
    placed_ref,
    lengths_ref,
    slot_of,
    sems,
):
    copies = [
        pltpu.make_async_copy(source, there, sems.at[i])
        for i, (source, there) in enumerate(
            ((parents_src, parents_ref), (placed_src, placed_ref), (lengths_src, lengths_ref))
        )
    ]
    for copy in copies:
        copy.start()
    for copy in copies:
        copy.wait()
    segments = parents_ref.shape[0]
    slot = lax.axis_index(SEG)
    own = placed_ref[slot]

    def place(j, carry):
        slot_of[placed_ref[j]] = j
        return carry

    lax.fori_loop(0, segments, place, 0)

    def clear(j, carry):
        meta_ref[j] = 0
        return carry

    lax.fori_loop(0, META, clear, 0)

    def above(state):
        seg, near, far, offset = state
        there = slot_of[seg]
        is_near = (there % 2 == slot % 2).astype(jnp.int32)
        entry = jnp.where(is_near == 1, NEAR + near, FAR + far)
        meta_ref[entry] = there
        meta_ref[LENGTHS + entry] = lengths_ref[seg]
        return parents_ref[seg], near + is_near, far + 1 - is_near, offset + lengths_ref[seg]

    zero = jnp.int32(0)
    _, near, far, offset = lax.while_loop(
        lambda state: state[0] >= 0, above, (parents_ref[own], zero, zero, zero)
    )
    meta_ref[0] = near
    meta_ref[1] = far
    index = lax.broadcasted_iota(jnp.int32, position_ref.shape, 1)
    position_ref[...] = (offset + index).astype(jnp.float32)
    span_ref[...] = (lengths_ref[own] - index).astype(jnp.float32)

    row = lax.broadcasted_iota(jnp.int32, (128, 128), 0)
    col = lax.broadcasted_iota(jnp.int32, (128, 128), 1)
    row_s = lax.broadcasted_iota(jnp.int32, (segments, 128), 0)
    col_s = lax.broadcasted_iota(jnp.int32, (segments, 128), 1)
    parent_of = jnp.full((segments, 128), -1, jnp.int32)
    held = jnp.full((segments, 128), -1, jnp.int32)
    for i in range(segments):
        parent_of = jnp.where(row_s == i, parents_ref[i], parent_of)
        held = jnp.where(row_s == i, placed_ref[i], held)
    step = jnp.where(parent_of == col_s, 1.0, 0.0)
    step = jnp.concatenate([step, jnp.zeros((128 - segments, 128), jnp.float32)], axis=0)
    ancestry = jnp.where(row == col, 1.0, 0.0) + step

    def times(a, b):
        return jnp.dot(
            a.astype(jnp.bfloat16), b.astype(jnp.bfloat16), preferred_element_type=jnp.float32
        )

    power = step
    reach = 1
    while 2 * reach <= segments:
        power = times(power, power)
        ancestry = ancestry + times(power, ancestry)
        reach *= 2
    children = jnp.sum(step, axis=0, keepdims=True)
    leafy = jnp.where((children < 0.5) & (col[:1] < segments), 1.0, 0.0)
    leaves = times(jnp.broadcast_to(leafy, (8, 128)), ancestry)[:1]
    placement = jnp.where(held == col_s, 1.0, 0.0)
    share = times(placement * leafy, ancestry)
    table_ref[...] = jnp.where(col_s < segments, share / jnp.maximum(leaves, 1.0), 0.0)


def weights_kernel(value_ref, readout_ref, key_ref, out_ref):
    quarters, part, rows = value_ref.shape
    value = value_ref[...].reshape(quarters * part, rows)
    readout = readout_ref[...].astype(jnp.bfloat16)
    folded = jnp.dot(readout, value, preferred_element_type=jnp.float32)
    high = folded.astype(jnp.bfloat16).astype(jnp.float32)
    low = folded - high
    width = key_ref.shape[0] - 8
    piece = jnp.concatenate([key_ref[:width], high, low, key_ref[width + 4 :]], axis=0)
    piece = piece.astype(jnp.bfloat16)
    for i in range(out_ref.shape[0]):
        out_ref[i] = piece


def masks_kernel(span_ref, live_ref, last_ref):
    live_ref[...] = jnp.where(span_ref[...] > 0.5, 1.0, 0.0)
    last_ref[...] = jnp.where(jnp.abs(span_ref[...] - 1.0) < 0.5, 1.0, 0.0)


def turned(raw, cosine, sine, axis):
    extent = raw.shape[axis]
    index = lax.broadcasted_iota(jnp.int32, raw.shape, axis)
    after = pltpu.roll(raw, extent - 1, axis)
    before = pltpu.roll(raw, 1, axis)
    return raw * cosine + jnp.where(index % 2 == 0, after, before) * sine


def half_projected(tokens_ref, weights_ref, total, parity):
    for even in range(2):

        @pl.when(parity == even)
        def _():
            blocks, _, depth = weights_ref.shape
            acc = total[...]
            for p in range(blocks):
                start = (2 * p + even) * depth
                acc += lax.dot_general(
                    weights_ref[p],
                    tokens_ref[:, start : start + depth],
                    (((1,), (1,)), ((), ())),
                    preferred_element_type=jnp.float32,
                )
            total[...] = acc


def near_keys_kernel(tokens_ref, weights_ref, out_ref):
    out_ref[...] = jnp.zeros_like(out_ref)
    half_projected(tokens_ref, weights_ref, out_ref, lax.axis_index("c"))


def far_keys_kernel(
    tokens_ref, weights_ref, near_ref, cosine_ref, sine_ref, out_ref, resid_ref, total
):
    total[...] = near_ref[...]
    half_projected(tokens_ref, weights_ref, total, 1 - lax.axis_index("c"))
    width = total.shape[0] - 8
    start = pl.multiple_of(lax.axis_index("x") * width, width)
    keys = turned(total[:width], cosine_ref[pl.ds(start, width)], sine_ref[pl.ds(start, width)], 0)
    last = total[width:]
    row = lax.broadcasted_iota(jnp.int32, last.shape, 0)
    summed = last + pltpu.roll(last, 6, 0)
    high = summed.astype(jnp.bfloat16).astype(jnp.float32)
    low = pltpu.roll(summed - high, 2, 0)
    tail = jnp.where(row < 2, high, jnp.where(row < 4, low, 0.0))
    resid_ref[...] = last[4:5]
    piece = jnp.concatenate([keys, tail], axis=0).astype(jnp.bfloat16)
    for i in range(out_ref.shape[0]):
        out_ref[i] = piece


def queries_kernel(tokens_ref, weights_ref, cosine_ref, sine_ref, out_ref, total):
    blocks, depth, _ = weights_ref.shape
    seg_len = tokens_ref.shape[0]
    half = lax.axis_index("zl")
    for upper in range(2):

        @pl.when(half == upper)
        def _():
            acc = jnp.zeros_like(total)
            for i in range(blocks):
                block = i // 4 * 4 + (i % 2 ^ upper) * 2 + i // 2 % 2
                acc += jnp.dot(
                    tokens_ref[:, block * depth : (block + 1) * depth],
                    weights_ref[i],
                    preferred_element_type=jnp.float32,
                )
            total[...] = acc

    raw = total[...].T
    for h in range(raw.shape[0] // HEAD_SIZE):
        head = raw[h * HEAD_SIZE : (h + 1) * HEAD_SIZE]
        out_ref[:, h * seg_len : (h + 1) * seg_len] = turned(
            head, cosine_ref[...], sine_ref[...], 0
        ).astype(jnp.bfloat16)


def spread_kernel(keys_ref, out_ref, sems):
    copies = [
        pltpu.make_async_copy(keys_ref, out_ref.at[i], sems.at[i]) for i in range(out_ref.shape[0])
    ]
    for copy in copies:
        copy.start()
    for copy in copies:
        copy.wait()


def scored(query_ref, keys_ref, slot):
    quarters = lax.axis_size("x")
    seg_len = keys_ref.shape[3]
    keys = keys_ref[pl.ds(slot // 2 % 2 * quarters, quarters), slot // 4]
    raw = lax.dot_general(
        keys.reshape(HEAD_SIZE, seg_len),
        query_ref[...],
        (((0,), (0,)), ((), ())),
        preferred_element_type=jnp.float32,
    )
    return raw * (HEAD_SIZE ** (-0.5) * LOG2_E)


def mixed_values(own_ref, other_ref, far, slot, weights):
    is_other = slot // 2 % 2 != lax.axis_index("zl")
    own, other = (ref[far, slot // 4].astype(jnp.float32) for ref in (own_ref, other_ref))
    return jnp.dot(
        jnp.where(is_other, other, own).astype(jnp.bfloat16),
        weights.astype(jnp.bfloat16),
        preferred_element_type=jnp.float32,
    )


def visit(meta_ref, far, query_ref, keys_ref, own_ref, other_ref, top, bottom, summed):
    key_at = lax.broadcasted_iota(jnp.int32, (keys_ref.shape[3], query_ref.shape[1]), 0)[:, :1]
    first = (NEAR, FAR)[far]

    def two(n, carry):
        entries = [first + 2 * n, first + 2 * n + 1]
        slots = [meta_ref[e] for e in entries]
        masked = [
            scored(query_ref, keys_ref, slot)
            + jnp.where(key_at < meta_ref[LENGTHS + e], 0.0, UNSEEN)
            for e, slot in zip(entries, slots)
        ]
        peak = jnp.max(jnp.maximum(masked[0], masked[1]), axis=0, keepdims=True)
        peak = jnp.maximum(top[...], peak)
        shrink = jnp.exp2(top[...] - peak)
        weights = [jnp.exp2(m - peak) for m in masked]
        top[...] = peak
        bottom[...] = bottom[...] * shrink + jnp.sum(
            weights[0] + weights[1], axis=0, keepdims=True
        )
        summed[...] = (
            summed[...] * shrink
            + mixed_values(own_ref, other_ref, far, slots[0], weights[0])
            + mixed_values(own_ref, other_ref, far, slots[1], weights[1])
        )
        return carry

    lax.fori_loop(0, (meta_ref[far] + 1) // 2, two, 0)


def near_kernel(meta_ref, query_ref, keys_ref, own_ref, other_ref, top, bottom, summed):
    seg_len = keys_ref.shape[3]
    shape = (seg_len, query_ref.shape[1])
    key_at = lax.broadcasted_iota(jnp.int32, shape, 0)
    query_at = lax.broadcasted_iota(jnp.int32, shape, 1) % seg_len
    own = lax.axis_index(SEG)
    masked = jnp.where(key_at <= query_at, scored(query_ref, keys_ref, own), UNSEEN)
    peak = jnp.max(masked, axis=0, keepdims=True)
    weights = jnp.exp2(masked - peak)
    top[...] = peak
    bottom[...] = jnp.sum(weights, axis=0, keepdims=True)
    summed[...] = mixed_values(own_ref, other_ref, 0, own, weights)
    visit(meta_ref, 0, query_ref, keys_ref, own_ref, other_ref, top, bottom, summed)


def far_kernel(
    meta_ref,
    query_ref,
    keys_ref,
    own_ref,
    other_ref,
    near_top,
    near_bottom,
    near_summed,
    out_ref,
    top,
    bottom,
    summed,
):
    top[...] = near_top[...]
    bottom[...] = near_bottom[...]
    summed[...] = near_summed[...]
    visit(meta_ref, 1, query_ref, keys_ref, own_ref, other_ref, top, bottom, summed)
    seg_len = keys_ref.shape[3]
    scaled = summed[...] / bottom[...]
    result = jnp.zeros((1, seg_len), jnp.float32)
    for h in range(query_ref.shape[1] // seg_len):
        part = scaled[:, h * seg_len : (h + 1) * seg_len]
        result += part[h : h + 1] + part[2 + h : 3 + h]
    for i in range(out_ref.shape[0]):
        out_ref[i] = result


def finish_kernel(parts_ref, resid_ref, live_ref, last_ref, out_ref, leaf_ref):
    total = resid_ref[...] + jnp.sum(parts_ref[...], axis=0)
    values = jnp.where(live_ref[...] > 0.5, total, 0.0)
    out_ref[...] = values
    leaf = jnp.sum(jnp.where(last_ref[...] > 0.5, values, 0.0), axis=1, keepdims=True)
    leaf_ref[...] = jnp.broadcast_to(leaf, leaf_ref.shape)


def gathered(value, axis):
    return lax.all_to_all(value, axis, 0, 0)


def on_device(
    tokens, w_query, key_weight, value_weight, resid_head, head_readout, parents, placed, lengths
):
    seg_len, model_width = tokens.shape
    segments = parents.shape[0]
    fsdp_size = lax.axis_size(FSDP)
    quarters = lax.axis_size("x")
    pairs = segments // 2
    width = key_weight.shape[1]
    rows = width + 8
    heads = w_query.shape[1] // HEAD_SIZE
    swap = [(0, 1), (1, 0)]
    params = pltpu.CompilerParams(vmem_limit_bytes=VMEM_LIMIT)

    sent = jnp.broadcast_to(value_weight.T[None], (quarters, width, seg_len))
    sent, w_query = lax.optimization_barrier((sent, w_query))
    other = lax.ppermute(w_query, "zl", swap)
    values_x = gathered(sent, "x")
    readout = head_readout.reshape(heads, HEAD_SIZE).astype(jnp.float32)
    own_readout = lax.dynamic_slice(
        resid_head, (lax.axis_index(SEG) * seg_len,), (seg_len,)
    )
    key_rows = jnp.concatenate(
        [
            jnp.pad(key_weight.T.astype(jnp.float32), ((0, 4), (0, 0))),
            jnp.pad(own_readout.astype(jnp.float32)[None], ((0, 3), (0, 0))),
        ]
    )
    both = jnp.pad(w_query, ((0, w_query.shape[0]), (0, 0)))
    values_x, other, readout, key_rows, both = lax.optimization_barrier(
        (values_x, other, readout, key_rows, both)
    )
    both = lax.dynamic_update_slice(both, other, (w_query.shape[0], 0))
    query_weight = lax.all_gather(both, ("y", "c"), axis=0, tiled=True)
    pieces = pl.pallas_call(
        weights_kernel,
        out_shape=jax.ShapeDtypeStruct((pairs, rows, seg_len), jnp.bfloat16),
        in_specs=[VMEM_SPEC] * 3,
        out_specs=VMEM_SPEC,
        compiler_params=params,
        name="fold_weights",
    )(values_x, readout, key_rows)

    near_weights = gathered(pieces, ("y", "zl"))
    by_token = jax.ShapeDtypeStruct((1, seg_len), jnp.float32)
    meta, table, positions, spans = pl.pallas_call(
        tree_kernel,
        out_shape=(
            jax.ShapeDtypeStruct((META,), jnp.int32),
            jax.ShapeDtypeStruct((segments, 128), jnp.float32),
            by_token,
            by_token,
        ),
        in_specs=[HBM_SPEC] * 3,
        out_specs=(SMEM_SPEC,) + (VMEM_SPEC,) * 3,
        scratch_shapes=[pltpu.SMEM((segments,), jnp.int32)] * 4
        + [pltpu.SemaphoreType.DMA((3,))],
        compiler_params=params,
        name="tree",
    )(parents, placed, lengths)
    dims = jnp.arange(HEAD_SIZE, dtype=jnp.int32)
    frequency = ROPE_BASE ** (-2.0 * (dims // 2).astype(jnp.float32) / HEAD_SIZE)
    angles = frequency[:, None] * positions
    cosine = jnp.cos(angles)
    sine = jnp.sin(angles) * jnp.where(dims % 2 == 0, -1.0, 1.0)[:, None]
    near_weights, cosine, sine, spans = lax.optimization_barrier(
        (near_weights, cosine, sine, spans)
    )

    far_weights = lax.ppermute(near_weights, "c", swap)
    live, last = pl.pallas_call(
        masks_kernel,
        out_shape=(by_token, by_token),
        in_specs=[VMEM_SPEC],
        out_specs=(VMEM_SPEC,) * 2,
        compiler_params=params,
        cost_estimate=pl.CostEstimate(flops=2**33, bytes_accessed=2**12, transcendentals=0),
        name="masks",
    )(spans)
    near_weights, live, last = lax.optimization_barrier((near_weights, live, last))
    near_sums = pl.pallas_call(
        near_keys_kernel,
        out_shape=jax.ShapeDtypeStruct((rows, seg_len), jnp.float32),
        in_specs=[VMEM_SPEC] * 2,
        out_specs=VMEM_SPEC,
        compiler_params=params,
        cost_estimate=pl.CostEstimate(
            flops=rows * seg_len * model_width, bytes_accessed=2**21, transcendentals=0
        ),
        name="project_near_keys",
    )(tokens, near_weights)
    far_weights, near_sums = lax.optimization_barrier((far_weights, near_sums))
    keys, residual = pl.pallas_call(
        far_keys_kernel,
        out_shape=(
            jax.ShapeDtypeStruct((lax.axis_size("y"), rows, seg_len), jnp.bfloat16),
            jax.ShapeDtypeStruct((1, seg_len), jnp.float32),
        ),
        in_specs=[VMEM_SPEC] * 5,
        out_specs=(VMEM_SPEC, VMEM_SPEC),
        scratch_shapes=[pltpu.VMEM((rows, seg_len), jnp.float32)],
        compiler_params=params,
        name="project_far_keys",
    )(tokens, far_weights, near_sums, cosine, sine)

    keys_y = gathered(keys, "y")
    spread = lax.axis_size(("zl", "x"))
    values = keys_y[:, width:]
    keys_y = keys_y[:, :width]
    copies = pl.pallas_call(
        spread_kernel,
        out_shape=jax.ShapeDtypeStruct((spread, *keys_y.shape), keys_y.dtype),
        in_specs=[VMEM_SPEC],
        out_specs=HBM_SPEC,
        scratch_shapes=[pltpu.SemaphoreType.DMA((spread,))],
        compiler_params=params,
        name="spread_keys",
    )(keys_y)
    near = gathered(copies, ("zl", "x"))
    values = jnp.stack([values, lax.ppermute(values, "c", swap)])
    values, query_sine = lax.optimization_barrier((values, sine))
    other_values = lax.ppermute(values, "zl", swap)
    queries = pl.pallas_call(
        queries_kernel,
        out_shape=jax.ShapeDtypeStruct((HEAD_SIZE, heads * seg_len), jnp.bfloat16),
        in_specs=[VMEM_SPEC] * 4,
        out_specs=VMEM_SPEC,
        scratch_shapes=[pltpu.VMEM((seg_len, heads * HEAD_SIZE), jnp.float32)],
        cost_estimate=pl.CostEstimate(
            flops=2 * seg_len * model_width * heads * HEAD_SIZE,
            bytes_accessed=2 * model_width * (seg_len + heads * HEAD_SIZE),
            transcendentals=0,
        ),
        compiler_params=params,
        name="project_queries",
    )(tokens, query_weight.reshape(segments, seg_len, -1), cosine, query_sine)
    near, queries, other_values = lax.optimization_barrier((near, queries, other_values))
    far = lax.ppermute(near, "c", swap)
    columns = heads * seg_len
    state = (
        jax.ShapeDtypeStruct((1, columns), jnp.float32),
        jax.ShapeDtypeStruct((1, columns), jnp.float32),
        jax.ShapeDtypeStruct((8, columns), jnp.float32),
    )
    near_state = pl.pallas_call(
        near_kernel,
        out_shape=state,
        in_specs=[SMEM_SPEC] + [VMEM_SPEC] * 4,
        out_specs=(VMEM_SPEC,) * 3,
        compiler_params=params,
        cost_estimate=pl.CostEstimate(
            flops=2**28, bytes_accessed=2**21, transcendentals=2**19
        ),
        name="attend_near",
    )(meta, queries, near, values, other_values)
    far, near_state = lax.optimization_barrier((far, near_state))
    mixed = pl.pallas_call(
        far_kernel,
        out_shape=jax.ShapeDtypeStruct((fsdp_size, 1, seg_len), jnp.float32),
        in_specs=[SMEM_SPEC] + [VMEM_SPEC] * 7,
        out_specs=VMEM_SPEC,
        scratch_shapes=[pltpu.VMEM(part.shape, part.dtype) for part in state],
        compiler_params=params,
        name="attend_far",
    )(meta, queries, far, values, other_values, *near_state)
    parts = gathered(mixed, FSDP)
    token_values, leaf_rows = pl.pallas_call(
        finish_kernel,
        out_shape=(
            jax.ShapeDtypeStruct((1, seg_len), jnp.float32),
            jax.ShapeDtypeStruct((segments, 128), jnp.float32),
        ),
        in_specs=[VMEM_SPEC] * 4,
        out_specs=(VMEM_SPEC, VMEM_SPEC),
        compiler_params=params,
        name="token_values",
    )(parts, residual, live, last)
    leaves = gathered(leaf_rows, SEG)
    branch = jnp.sum(leaves * table, axis=0)[:segments]
    return (token_values.reshape(seg_len), branch)


def solution(mesh):
    fine = Mesh(mesh.devices.reshape(8, 2, 2, 4, 4), SEG + FSDP)
    in_specs = (
        P(SEG, None),
        P(SEG, FSDP),
        P(SEG, FSDP),
        P(SEG, FSDP),
        P(),
        P(FSDP),
        P(),
        P(),
        P(),
    )
    out_specs = (P(SEG), P())
    return jax.shard_map(
        on_device, mesh=fine, in_specs=in_specs, out_specs=out_specs, check_vma=False
    )
```

```python
import jax
import jax.numpy as jnp
from jax import lax
from jax.experimental import pallas as pl
from jax.experimental.pallas import tpu as pltpu
from jax.sharding import Mesh
from jax.sharding import PartitionSpec as P

KEY_VALUE_HEADS = 4
HEAD_SIZE = 128
ROPE_BASE = 1000000.0
SEG = ("y", "zl", "c")
FSDP = ("zh", "x")
NEAR, FAR, LENGTHS, META = 8, 48, 80, 168
UNSEEN = -1e30
LOG2_E = 1.4426950408889634
VMEM_LIMIT = 40 * 1024 * 1024

VMEM_SPEC = pl.BlockSpec(memory_space=pltpu.VMEM)
SMEM_SPEC = pl.BlockSpec(memory_space=pltpu.SMEM)
HBM_SPEC = pl.BlockSpec(memory_space=pltpu.HBM)


def tree_kernel(
    parents_src,
    placed_src,
    lengths_src,
    meta_ref,
    table_ref,
    position_ref,
    span_ref,
    parents_ref,
    placed_ref,
    lengths_ref,
    slot_of,
    sems,
):
    copies = [
        pltpu.make_async_copy(source, there, sems.at[i])
        for i, (source, there) in enumerate(
            ((parents_src, parents_ref), (placed_src, placed_ref), (lengths_src, lengths_ref))
        )
    ]
    for copy in copies:
        copy.start()
    for copy in copies:
        copy.wait()
    segments = parents_ref.shape[0]
    slot = lax.axis_index(SEG)
    own = placed_ref[slot]

    def place(j, carry):
        slot_of[placed_ref[j]] = j
        return carry

    lax.fori_loop(0, segments, place, 0)

    def clear(j, carry):
        meta_ref[j] = 0
        return carry

    lax.fori_loop(0, META, clear, 0)

    def above(state):
        seg, near, far, offset = state
        there = slot_of[seg]
        is_near = (there % 2 == slot % 2).astype(jnp.int32)
        entry = jnp.where(is_near == 1, NEAR + near, FAR + far)
        meta_ref[entry] = there
        meta_ref[LENGTHS + entry] = lengths_ref[seg]
        return parents_ref[seg], near + is_near, far + 1 - is_near, offset + lengths_ref[seg]

    zero = jnp.int32(0)
    _, near, far, offset = lax.while_loop(
        lambda state: state[0] >= 0, above, (parents_ref[own], zero, zero, zero)
    )
    meta_ref[0] = near
    meta_ref[1] = far
    index = lax.broadcasted_iota(jnp.int32, position_ref.shape, 1)
    position_ref[...] = (offset + index).astype(jnp.float32)
    span_ref[...] = (lengths_ref[own] - index).astype(jnp.float32)

    row = lax.broadcasted_iota(jnp.int32, (128, 128), 0)
    col = lax.broadcasted_iota(jnp.int32, (128, 128), 1)
    row_s = lax.broadcasted_iota(jnp.int32, (segments, 128), 0)
    col_s = lax.broadcasted_iota(jnp.int32, (segments, 128), 1)
    parent_of = jnp.full((segments, 128), -1, jnp.int32)
    held = jnp.full((segments, 128), -1, jnp.int32)
    for i in range(segments):
        parent_of = jnp.where(row_s == i, parents_ref[i], parent_of)
        held = jnp.where(row_s == i, placed_ref[i], held)
    step = jnp.where(parent_of == col_s, 1.0, 0.0)
    step = jnp.concatenate([step, jnp.zeros((128 - segments, 128), jnp.float32)], axis=0)
    ancestry = jnp.where(row == col, 1.0, 0.0) + step

    def times(a, b):
        return jnp.dot(
            a.astype(jnp.bfloat16), b.astype(jnp.bfloat16), preferred_element_type=jnp.float32
        )

    power = step
    reach = 1
    while 2 * reach <= segments:
        power = times(power, power)
        ancestry = ancestry + times(power, ancestry)
        reach *= 2
    children = jnp.sum(step, axis=0, keepdims=True)
    leafy = jnp.where((children < 0.5) & (col[:1] < segments), 1.0, 0.0)
    leaves = times(jnp.broadcast_to(leafy, (8, 128)), ancestry)[:1]
    placement = jnp.where(held == col_s, 1.0, 0.0)
    share = times(placement * leafy, ancestry)
    table_ref[...] = jnp.where(col_s < segments, share / jnp.maximum(leaves, 1.0), 0.0)


def weights_kernel(value_ref, readout_ref, key_ref, out_ref):
    quarters, part, rows = value_ref.shape
    value = value_ref[...].reshape(quarters * part, rows)
    readout = readout_ref[...].astype(jnp.bfloat16)
    folded = jnp.dot(readout, value, preferred_element_type=jnp.float32)
    high = folded.astype(jnp.bfloat16).astype(jnp.float32)
    low = folded - high
    width = key_ref.shape[0] - 8
    piece = jnp.concatenate([key_ref[:width], high, low, key_ref[width + 4 :]], axis=0)
    piece = piece.astype(jnp.bfloat16)
    for i in range(out_ref.shape[0]):
        out_ref[i] = piece


def masks_kernel(span_ref, live_ref, last_ref):
    live_ref[...] = jnp.where(span_ref[...] > 0.5, 1.0, 0.0)
    last_ref[...] = jnp.where(jnp.abs(span_ref[...] - 1.0) < 0.5, 1.0, 0.0)


def turned(raw, cosine, sine, axis):
    extent = raw.shape[axis]
    index = lax.broadcasted_iota(jnp.int32, raw.shape, axis)
    after = pltpu.roll(raw, extent - 1, axis)
    before = pltpu.roll(raw, 1, axis)
    return raw * cosine + jnp.where(index % 2 == 0, after, before) * sine


def half_projected(tokens_ref, weights_ref, total, parity):
    for even in range(2):

        @pl.when(parity == even)
        def _():
            blocks, _, depth = weights_ref.shape
            acc = total[...]
            for p in range(blocks):
                start = (2 * p + even) * depth
                acc += lax.dot_general(
                    weights_ref[p],
                    tokens_ref[:, start : start + depth],
                    (((1,), (1,)), ((), ())),
                    preferred_element_type=jnp.float32,
                )
            total[...] = acc


def near_keys_kernel(tokens_ref, weights_ref, out_ref):
    out_ref[...] = jnp.zeros_like(out_ref)
    half_projected(tokens_ref, weights_ref, out_ref, lax.axis_index("c"))


def far_keys_kernel(
    tokens_ref, weights_ref, near_ref, cosine_ref, sine_ref, out_ref, resid_ref, total
):
    total[...] = near_ref[...]
    half_projected(tokens_ref, weights_ref, total, 1 - lax.axis_index("c"))
    width = total.shape[0] - 8
    start = pl.multiple_of(lax.axis_index("x") * width, width)
    keys = turned(total[:width], cosine_ref[pl.ds(start, width)], sine_ref[pl.ds(start, width)], 0)
    last = total[width:]
    row = lax.broadcasted_iota(jnp.int32, last.shape, 0)
    summed = last + pltpu.roll(last, 6, 0)
    high = summed.astype(jnp.bfloat16).astype(jnp.float32)
    low = pltpu.roll(summed - high, 2, 0)
    tail = jnp.where(row < 2, high, jnp.where(row < 4, low, 0.0))
    resid_ref[...] = last[4:5]
    piece = jnp.concatenate([keys, tail], axis=0).astype(jnp.bfloat16)
    for i in range(out_ref.shape[0]):
        out_ref[i] = piece


def queries_kernel(tokens_ref, weights_ref, cosine_ref, sine_ref, out_ref, total):
    blocks, depth, _ = weights_ref.shape
    seg_len = tokens_ref.shape[0]
    half = lax.axis_index("zl")
    for upper in range(2):

        @pl.when(half == upper)
        def _():
            acc = jnp.zeros_like(total)
            for i in range(blocks):
                block = i // 4 * 4 + (i % 2 ^ upper) * 2 + i // 2 % 2
                acc += jnp.dot(
                    tokens_ref[:, block * depth : (block + 1) * depth],
                    weights_ref[i],
                    preferred_element_type=jnp.float32,
                )
            total[...] = acc

    raw = total[...].T
    for h in range(raw.shape[0] // HEAD_SIZE):
        head = raw[h * HEAD_SIZE : (h + 1) * HEAD_SIZE]
        out_ref[:, h * seg_len : (h + 1) * seg_len] = turned(
            head, cosine_ref[...], sine_ref[...], 0
        ).astype(jnp.bfloat16)


def spread_kernel(keys_ref, out_ref, sems):
    copies = [
        pltpu.make_async_copy(keys_ref, out_ref.at[i], sems.at[i]) for i in range(out_ref.shape[0])
    ]
    for copy in copies:
        copy.start()
    for copy in copies:
        copy.wait()


def scored(query_ref, keys_ref, slot):
    quarters = lax.axis_size("x")
    seg_len = keys_ref.shape[3]
    keys = keys_ref[pl.ds(slot // 2 % 2 * quarters, quarters), slot // 4]
    raw = lax.dot_general(
        keys.reshape(HEAD_SIZE, seg_len),
        query_ref[...],
        (((0,), (0,)), ((), ())),
        preferred_element_type=jnp.float32,
    )
    return raw * (HEAD_SIZE ** (-0.5) * LOG2_E)


def mixed_values(own_ref, other_ref, far, slot, weights):
    is_other = slot // 2 % 2 != lax.axis_index("zl")
    own, other = (ref[far, slot // 4].astype(jnp.float32) for ref in (own_ref, other_ref))
    return jnp.dot(
        jnp.where(is_other, other, own).astype(jnp.bfloat16),
        weights.astype(jnp.bfloat16),
        preferred_element_type=jnp.float32,
    )


def visit(meta_ref, far, query_ref, keys_ref, own_ref, other_ref, top, bottom, summed):
    key_at = lax.broadcasted_iota(jnp.int32, (keys_ref.shape[3], query_ref.shape[1]), 0)[:, :1]
    first = (NEAR, FAR)[far]

    def two(n, carry):
        entries = [first + 2 * n, first + 2 * n + 1]
        slots = [meta_ref[e] for e in entries]
        masked = [
            scored(query_ref, keys_ref, slot)
            + jnp.where(key_at < meta_ref[LENGTHS + e], 0.0, UNSEEN)
            for e, slot in zip(entries, slots)
        ]
        peak = jnp.max(jnp.maximum(masked[0], masked[1]), axis=0, keepdims=True)
        peak = jnp.maximum(top[...], peak)
        shrink = jnp.exp2(top[...] - peak)
        weights = [jnp.exp2(m - peak) for m in masked]
        top[...] = peak
        bottom[...] = bottom[...] * shrink + jnp.sum(
            weights[0] + weights[1], axis=0, keepdims=True
        )
        summed[...] = (
            summed[...] * shrink
            + mixed_values(own_ref, other_ref, far, slots[0], weights[0])
            + mixed_values(own_ref, other_ref, far, slots[1], weights[1])
        )
        return carry

    lax.fori_loop(0, (meta_ref[far] + 1) // 2, two, 0)


def near_kernel(meta_ref, query_ref, keys_ref, own_ref, other_ref, top, bottom, summed):
    seg_len = keys_ref.shape[3]
    shape = (seg_len, query_ref.shape[1])
    key_at = lax.broadcasted_iota(jnp.int32, shape, 0)
    query_at = lax.broadcasted_iota(jnp.int32, shape, 1) % seg_len
    own = lax.axis_index(SEG)
    masked = jnp.where(key_at <= query_at, scored(query_ref, keys_ref, own), UNSEEN)
    peak = jnp.max(masked, axis=0, keepdims=True)
    weights = jnp.exp2(masked - peak)
    top[...] = peak
    bottom[...] = jnp.sum(weights, axis=0, keepdims=True)
    summed[...] = mixed_values(own_ref, other_ref, 0, own, weights)
    visit(meta_ref, 0, query_ref, keys_ref, own_ref, other_ref, top, bottom, summed)


def far_kernel(
    meta_ref,
    query_ref,
    keys_ref,
    own_ref,
    other_ref,
    near_top,
    near_bottom,
    near_summed,
    out_ref,
    top,
    bottom,
    summed,
):
    top[...] = near_top[...]
    bottom[...] = near_bottom[...]
    summed[...] = near_summed[...]
    visit(meta_ref, 1, query_ref, keys_ref, own_ref, other_ref, top, bottom, summed)
    seg_len = keys_ref.shape[3]
    scaled = summed[...] / bottom[...]
    result = jnp.zeros((1, seg_len), jnp.float32)
    for h in range(query_ref.shape[1] // seg_len):
        part = scaled[:, h * seg_len : (h + 1) * seg_len]
        result += part[h : h + 1] + part[2 + h : 3 + h]
    for i in range(out_ref.shape[0]):
        out_ref[i] = result


def finish_kernel(parts_ref, resid_ref, live_ref, last_ref, out_ref, leaf_ref):
    total = resid_ref[...] + jnp.sum(parts_ref[...], axis=0)
    values = jnp.where(live_ref[...] > 0.5, total, 0.0)
    out_ref[...] = values
    leaf = jnp.sum(jnp.where(last_ref[...] > 0.5, values, 0.0), axis=1, keepdims=True)
    leaf_ref[...] = jnp.broadcast_to(leaf, leaf_ref.shape)


def gathered(value, axis):
    return lax.all_to_all(value, axis, 0, 0)


def on_device(
    tokens, w_query, key_weight, value_weight, resid_head, head_readout, parents, placed, lengths
):
    seg_len, model_width = tokens.shape
    segments = parents.shape[0]
    fsdp_size = lax.axis_size(FSDP)
    quarters = lax.axis_size("x")
    pairs = segments // 2
    width = key_weight.shape[1]
    rows = width + 8
    heads = w_query.shape[1] // HEAD_SIZE
    swap = [(0, 1), (1, 0)]
    params = pltpu.CompilerParams(vmem_limit_bytes=VMEM_LIMIT)

    sent = jnp.broadcast_to(value_weight.T[None], (quarters, width, seg_len))
    sent, w_query = lax.optimization_barrier((sent, w_query))
    other = lax.ppermute(w_query, "zl", swap)
    values_x = gathered(sent, "x")
    readout = head_readout.reshape(heads, HEAD_SIZE).astype(jnp.float32)
    own_readout = lax.dynamic_slice(
        resid_head, (lax.axis_index(SEG) * seg_len,), (seg_len,)
    )
    key_rows = jnp.concatenate(
        [
            jnp.pad(key_weight.T.astype(jnp.float32), ((0, 4), (0, 0))),
            jnp.pad(own_readout.astype(jnp.float32)[None], ((0, 3), (0, 0))),
        ]
    )
    both = jnp.pad(w_query, ((0, w_query.shape[0]), (0, 0)))
    values_x, other, readout, key_rows, both = lax.optimization_barrier(
        (values_x, other, readout, key_rows, both)
    )
    both = lax.dynamic_update_slice(both, other, (w_query.shape[0], 0))
    pieces = pl.pallas_call(
        weights_kernel,
        out_shape=jax.ShapeDtypeStruct((pairs, rows, seg_len), jnp.bfloat16),
        in_specs=[VMEM_SPEC] * 3,
        out_specs=VMEM_SPEC,
        compiler_params=params,
        cost_estimate=pl.CostEstimate(flops=2**33, bytes_accessed=2**12, transcendentals=0),
        name="fold_weights",
    )(values_x, readout, key_rows)
    pieces, both = lax.optimization_barrier((pieces, both))
    query_weight = lax.all_gather(both, ("y", "c"), axis=0, tiled=True)

    near_weights = gathered(pieces, ("y", "zl"))
    by_token = jax.ShapeDtypeStruct((1, seg_len), jnp.float32)
    meta, table, positions, spans = pl.pallas_call(
        tree_kernel,
        out_shape=(
            jax.ShapeDtypeStruct((META,), jnp.int32),
            jax.ShapeDtypeStruct((segments, 128), jnp.float32),
            by_token,
            by_token,
        ),
        in_specs=[HBM_SPEC] * 3,
        out_specs=(SMEM_SPEC,) + (VMEM_SPEC,) * 3,
        scratch_shapes=[pltpu.SMEM((segments,), jnp.int32)] * 4
        + [pltpu.SemaphoreType.DMA((3,))],
        compiler_params=params,
        name="tree",
    )(parents, placed, lengths)
    dims = jnp.arange(HEAD_SIZE, dtype=jnp.int32)
    frequency = ROPE_BASE ** (-2.0 * (dims // 2).astype(jnp.float32) / HEAD_SIZE)
    angles = frequency[:, None] * positions
    cosine = jnp.cos(angles)
    sine = jnp.sin(angles) * jnp.where(dims % 2 == 0, -1.0, 1.0)[:, None]
    near_weights, cosine, sine, spans = lax.optimization_barrier(
        (near_weights, cosine, sine, spans)
    )

    far_weights = lax.ppermute(near_weights, "c", swap)
    live, last = pl.pallas_call(
        masks_kernel,
        out_shape=(by_token, by_token),
        in_specs=[VMEM_SPEC],
        out_specs=(VMEM_SPEC,) * 2,
        compiler_params=params,
        cost_estimate=pl.CostEstimate(flops=2**33, bytes_accessed=2**12, transcendentals=0),
        name="masks",
    )(spans)
    near_weights, live, last = lax.optimization_barrier((near_weights, live, last))
    near_sums = pl.pallas_call(
        near_keys_kernel,
        out_shape=jax.ShapeDtypeStruct((rows, seg_len), jnp.float32),
        in_specs=[VMEM_SPEC] * 2,
        out_specs=VMEM_SPEC,
        compiler_params=params,
        cost_estimate=pl.CostEstimate(
            flops=rows * seg_len * model_width, bytes_accessed=2**21, transcendentals=0
        ),
        name="project_near_keys",
    )(tokens, near_weights)
    far_weights, near_sums = lax.optimization_barrier((far_weights, near_sums))
    keys, residual = pl.pallas_call(
        far_keys_kernel,
        out_shape=(
            jax.ShapeDtypeStruct((lax.axis_size("y"), rows, seg_len), jnp.bfloat16),
            jax.ShapeDtypeStruct((1, seg_len), jnp.float32),
        ),
        in_specs=[VMEM_SPEC] * 5,
        out_specs=(VMEM_SPEC, VMEM_SPEC),
        scratch_shapes=[pltpu.VMEM((rows, seg_len), jnp.float32)],
        compiler_params=params,
        name="project_far_keys",
    )(tokens, far_weights, near_sums, cosine, sine)

    keys_y = gathered(keys, "y")
    spread = lax.axis_size(("zl", "x"))
    values = keys_y[:, width:]
    keys_y = keys_y[:, :width]
    copies = pl.pallas_call(
        spread_kernel,
        out_shape=jax.ShapeDtypeStruct((spread, *keys_y.shape), keys_y.dtype),
        in_specs=[VMEM_SPEC],
        out_specs=HBM_SPEC,
        scratch_shapes=[pltpu.SemaphoreType.DMA((spread,))],
        compiler_params=params,
        name="spread_keys",
    )(keys_y)
    near = gathered(copies, ("zl", "x"))
    values = jnp.stack([values, lax.ppermute(values, "c", swap)])
    values, query_sine = lax.optimization_barrier((values, sine))
    other_values = lax.ppermute(values, "zl", swap)
    queries = pl.pallas_call(
        queries_kernel,
        out_shape=jax.ShapeDtypeStruct((HEAD_SIZE, heads * seg_len), jnp.bfloat16),
        in_specs=[VMEM_SPEC] * 4,
        out_specs=VMEM_SPEC,
        scratch_shapes=[pltpu.VMEM((seg_len, heads * HEAD_SIZE), jnp.float32)],
        cost_estimate=pl.CostEstimate(
            flops=2 * seg_len * model_width * heads * HEAD_SIZE,
            bytes_accessed=2 * model_width * (seg_len + heads * HEAD_SIZE),
            transcendentals=0,
        ),
        compiler_params=params,
        name="project_queries",
    )(tokens, query_weight.reshape(segments, seg_len, -1), cosine, query_sine)
    near, queries, other_values = lax.optimization_barrier((near, queries, other_values))
    far = lax.ppermute(near, "c", swap)
    columns = heads * seg_len
    state = (
        jax.ShapeDtypeStruct((1, columns), jnp.float32),
        jax.ShapeDtypeStruct((1, columns), jnp.float32),
        jax.ShapeDtypeStruct((8, columns), jnp.float32),
    )
    near_state = pl.pallas_call(
        near_kernel,
        out_shape=state,
        in_specs=[SMEM_SPEC] + [VMEM_SPEC] * 4,
        out_specs=(VMEM_SPEC,) * 3,
        compiler_params=params,
        cost_estimate=pl.CostEstimate(
            flops=2**28, bytes_accessed=2**21, transcendentals=2**19
        ),
        name="attend_near",
    )(meta, queries, near, values, other_values)
    far, near_state = lax.optimization_barrier((far, near_state))
    mixed = pl.pallas_call(
        far_kernel,
        out_shape=jax.ShapeDtypeStruct((fsdp_size, 1, seg_len), jnp.float32),
        in_specs=[SMEM_SPEC] + [VMEM_SPEC] * 7,
        out_specs=VMEM_SPEC,
        scratch_shapes=[pltpu.VMEM(part.shape, part.dtype) for part in state],
        compiler_params=params,
        name="attend_far",
    )(meta, queries, far, values, other_values, *near_state)
    parts = gathered(mixed, FSDP)
    token_values, leaf_rows = pl.pallas_call(
        finish_kernel,
        out_shape=(
            jax.ShapeDtypeStruct((1, seg_len), jnp.float32),
            jax.ShapeDtypeStruct((segments, 128), jnp.float32),
        ),
        in_specs=[VMEM_SPEC] * 4,
        out_specs=(VMEM_SPEC, VMEM_SPEC),
        compiler_params=params,
        name="token_values",
    )(parts, residual, live, last)
    leaves = gathered(leaf_rows, SEG)
    branch = jnp.sum(leaves * table, axis=0)[:segments]
    return (token_values.reshape(seg_len), branch)


def solution(mesh):
    fine = Mesh(mesh.devices.reshape(8, 2, 2, 4, 4), SEG + FSDP)
    in_specs = (
        P(SEG, None),
        P(SEG, FSDP),
        P(SEG, FSDP),
        P(SEG, FSDP),
        P(),
        P(FSDP),
        P(),
        P(),
        P(),
    )
    out_specs = (P(SEG), P())
    return jax.shard_map(
        on_device, mesh=fine, in_specs=in_specs, out_specs=out_specs, check_vma=False
    )
```

```python
import jax
import jax.numpy as jnp
from jax import lax
from jax.experimental import pallas as pl
from jax.experimental.pallas import tpu as pltpu
from jax.sharding import Mesh
from jax.sharding import PartitionSpec as P

KEY_VALUE_HEADS = 4
HEAD_SIZE = 128
ROPE_BASE = 1000000.0
SEG = ("y", "zl", "c")
FSDP = ("zh", "x")
NEAR, FAR, LENGTHS, META = 8, 48, 80, 168
UNSEEN = -1e30
LOG2_E = 1.4426950408889634
VMEM_LIMIT = 40 * 1024 * 1024

VMEM_SPEC = pl.BlockSpec(memory_space=pltpu.VMEM)
SMEM_SPEC = pl.BlockSpec(memory_space=pltpu.SMEM)
HBM_SPEC = pl.BlockSpec(memory_space=pltpu.HBM)


def tree_kernel(
    parents_src,
    placed_src,
    lengths_src,
    meta_ref,
    table_ref,
    position_ref,
    span_ref,
    parents_ref,
    placed_ref,
    lengths_ref,
    slot_of,
    sems,
):
    copies = [
        pltpu.make_async_copy(source, there, sems.at[i])
        for i, (source, there) in enumerate(
            ((parents_src, parents_ref), (placed_src, placed_ref), (lengths_src, lengths_ref))
        )
    ]
    for copy in copies:
        copy.start()
    for copy in copies:
        copy.wait()
    segments = parents_ref.shape[0]
    slot = lax.axis_index(SEG)
    own = placed_ref[slot]

    def place(j, carry):
        slot_of[placed_ref[j]] = j
        return carry

    lax.fori_loop(0, segments, place, 0)

    def clear(j, carry):
        meta_ref[j] = 0
        return carry

    lax.fori_loop(0, META, clear, 0)

    def above(state):
        seg, near, far, offset = state
        there = slot_of[seg]
        is_near = (there % 2 == slot % 2).astype(jnp.int32)
        entry = jnp.where(is_near == 1, NEAR + near, FAR + far)
        meta_ref[entry] = there
        meta_ref[LENGTHS + entry] = lengths_ref[seg]
        return parents_ref[seg], near + is_near, far + 1 - is_near, offset + lengths_ref[seg]

    zero = jnp.int32(0)
    _, near, far, offset = lax.while_loop(
        lambda state: state[0] >= 0, above, (parents_ref[own], zero, zero, zero)
    )
    meta_ref[0] = near
    meta_ref[1] = far
    index = lax.broadcasted_iota(jnp.int32, position_ref.shape, 1)
    position_ref[...] = (offset + index).astype(jnp.float32)
    span_ref[...] = (lengths_ref[own] - index).astype(jnp.float32)

    row = lax.broadcasted_iota(jnp.int32, (128, 128), 0)
    col = lax.broadcasted_iota(jnp.int32, (128, 128), 1)
    row_s = lax.broadcasted_iota(jnp.int32, (segments, 128), 0)
    col_s = lax.broadcasted_iota(jnp.int32, (segments, 128), 1)
    parent_of = jnp.full((segments, 128), -1, jnp.int32)
    held = jnp.full((segments, 128), -1, jnp.int32)
    for i in range(segments):
        parent_of = jnp.where(row_s == i, parents_ref[i], parent_of)
        held = jnp.where(row_s == i, placed_ref[i], held)
    step = jnp.where(parent_of == col_s, 1.0, 0.0)
    step = jnp.concatenate([step, jnp.zeros((128 - segments, 128), jnp.float32)], axis=0)
    ancestry = jnp.where(row == col, 1.0, 0.0) + step

    def times(a, b):
        return jnp.dot(
            a.astype(jnp.bfloat16), b.astype(jnp.bfloat16), preferred_element_type=jnp.float32
        )

    power = step
    reach = 1
    while 2 * reach <= segments:
        power = times(power, power)
        ancestry = ancestry + times(power, ancestry)
        reach *= 2
    children = jnp.sum(step, axis=0, keepdims=True)
    leafy = jnp.where((children < 0.5) & (col[:1] < segments), 1.0, 0.0)
    leaves = times(jnp.broadcast_to(leafy, (8, 128)), ancestry)[:1]
    placement = jnp.where(held == col_s, 1.0, 0.0)
    share = times(placement * leafy, ancestry)
    table_ref[...] = jnp.where(col_s < segments, share / jnp.maximum(leaves, 1.0), 0.0)


def weights_kernel(value_ref, readout_ref, key_ref, out_ref):
    quarters, part, rows = value_ref.shape
    value = value_ref[...].reshape(quarters * part, rows)
    readout = readout_ref[...].astype(jnp.bfloat16)
    folded = jnp.dot(readout, value, preferred_element_type=jnp.float32)
    high = folded.astype(jnp.bfloat16).astype(jnp.float32)
    low = folded - high
    width = key_ref.shape[0] - 8
    piece = jnp.concatenate([key_ref[:width], high, low, key_ref[width + 4 :]], axis=0)
    piece = piece.astype(jnp.bfloat16)
    for i in range(out_ref.shape[0]):
        out_ref[i] = piece


def masks_kernel(span_ref, live_ref, last_ref):
    live_ref[...] = jnp.where(span_ref[...] > 0.5, 1.0, 0.0)
    last_ref[...] = jnp.where(jnp.abs(span_ref[...] - 1.0) < 0.5, 1.0, 0.0)


def turned(raw, cosine, sine, axis):
    extent = raw.shape[axis]
    index = lax.broadcasted_iota(jnp.int32, raw.shape, axis)
    after = pltpu.roll(raw, extent - 1, axis)
    before = pltpu.roll(raw, 1, axis)
    return raw * cosine + jnp.where(index % 2 == 0, after, before) * sine


def half_projected(tokens_ref, weights_ref, total, parity):
    for even in range(2):

        @pl.when(parity == even)
        def _():
            blocks, _, depth = weights_ref.shape
            acc = total[...]
            for p in range(blocks):
                start = (2 * p + even) * depth
                acc += lax.dot_general(
                    weights_ref[p],
                    tokens_ref[:, start : start + depth],
                    (((1,), (1,)), ((), ())),
                    preferred_element_type=jnp.float32,
                )
            total[...] = acc


def near_keys_kernel(tokens_ref, weights_ref, out_ref):
    out_ref[...] = jnp.zeros_like(out_ref)
    half_projected(tokens_ref, weights_ref, out_ref, lax.axis_index("c"))


def far_keys_kernel(
    tokens_ref, weights_ref, near_ref, cosine_ref, sine_ref, out_ref, resid_ref, total
):
    total[...] = near_ref[...]
    half_projected(tokens_ref, weights_ref, total, 1 - lax.axis_index("c"))
    width = total.shape[0] - 8
    start = pl.multiple_of(lax.axis_index("x") * width, width)
    keys = turned(total[:width], cosine_ref[pl.ds(start, width)], sine_ref[pl.ds(start, width)], 0)
    last = total[width:]
    row = lax.broadcasted_iota(jnp.int32, last.shape, 0)
    summed = last + pltpu.roll(last, 6, 0)
    high = summed.astype(jnp.bfloat16).astype(jnp.float32)
    low = pltpu.roll(summed - high, 2, 0)
    tail = jnp.where(row < 2, high, jnp.where(row < 4, low, 0.0))
    resid_ref[...] = last[4:5]
    piece = jnp.concatenate([keys, tail], axis=0).astype(jnp.bfloat16)
    for i in range(out_ref.shape[0]):
        out_ref[i] = piece


def queries_kernel(tokens_ref, weights_ref, cosine_ref, sine_ref, out_ref, total):
    blocks, depth, _ = weights_ref.shape
    seg_len = tokens_ref.shape[0]
    half = lax.axis_index("zl")
    for upper in range(2):

        @pl.when(half == upper)
        def _():
            acc = jnp.zeros_like(total)
            for i in range(blocks):
                block = i // 4 * 4 + (i % 2 ^ upper) * 2 + i // 2 % 2
                acc += jnp.dot(
                    tokens_ref[:, block * depth : (block + 1) * depth],
                    weights_ref[i],
                    preferred_element_type=jnp.float32,
                )
            total[...] = acc

    raw = total[...].T
    for h in range(raw.shape[0] // HEAD_SIZE):
        head = raw[h * HEAD_SIZE : (h + 1) * HEAD_SIZE]
        out_ref[:, h * seg_len : (h + 1) * seg_len] = turned(
            head, cosine_ref[...], sine_ref[...], 0
        ).astype(jnp.bfloat16)


def spread_kernel(keys_ref, out_ref, sems):
    copies = [
        pltpu.make_async_copy(keys_ref, out_ref.at[i], sems.at[i]) for i in range(out_ref.shape[0])
    ]
    for copy in copies:
        copy.start()
    for copy in copies:
        copy.wait()


def scored(query_ref, keys_ref, slot):
    quarters = lax.axis_size("x")
    seg_len = keys_ref.shape[3]
    keys = keys_ref[pl.ds(slot // 2 % 2 * quarters, quarters), slot // 4]
    raw = lax.dot_general(
        keys.reshape(HEAD_SIZE, seg_len),
        query_ref[...],
        (((0,), (0,)), ((), ())),
        preferred_element_type=jnp.float32,
    )
    return raw * (HEAD_SIZE ** (-0.5) * LOG2_E)


def mixed_values(own_ref, other_ref, far, slot, weights):
    is_other = slot // 2 % 2 != lax.axis_index("zl")
    own, other = (ref[far, slot // 4].astype(jnp.float32) for ref in (own_ref, other_ref))
    return jnp.dot(
        jnp.where(is_other, other, own).astype(jnp.bfloat16),
        weights.astype(jnp.bfloat16),
        preferred_element_type=jnp.float32,
    )


def visit(meta_ref, far, query_ref, keys_ref, own_ref, other_ref, top, bottom, summed):
    key_at = lax.broadcasted_iota(jnp.int32, (keys_ref.shape[3], query_ref.shape[1]), 0)[:, :1]
    first = (NEAR, FAR)[far]

    def two(n, carry):
        entries = [first + 2 * n, first + 2 * n + 1]
        slots = [meta_ref[e] for e in entries]
        masked = [
            scored(query_ref, keys_ref, slot)
            + jnp.where(key_at < meta_ref[LENGTHS + e], 0.0, UNSEEN)
            for e, slot in zip(entries, slots)
        ]
        peak = jnp.max(jnp.maximum(masked[0], masked[1]), axis=0, keepdims=True)
        peak = jnp.maximum(top[...], peak)
        shrink = jnp.exp2(top[...] - peak)
        weights = [jnp.exp2(m - peak) for m in masked]
        top[...] = peak
        bottom[...] = bottom[...] * shrink + jnp.sum(
            weights[0] + weights[1], axis=0, keepdims=True
        )
        summed[...] = (
            summed[...] * shrink
            + mixed_values(own_ref, other_ref, far, slots[0], weights[0])
            + mixed_values(own_ref, other_ref, far, slots[1], weights[1])
        )
        return carry

    lax.fori_loop(0, (meta_ref[far] + 1) // 2, two, 0)


def near_kernel(meta_ref, query_ref, keys_ref, own_ref, other_ref, top, bottom, summed):
    seg_len = keys_ref.shape[3]
    shape = (seg_len, query_ref.shape[1])
    key_at = lax.broadcasted_iota(jnp.int32, shape, 0)
    query_at = lax.broadcasted_iota(jnp.int32, shape, 1) % seg_len
    own = lax.axis_index(SEG)
    masked = jnp.where(key_at <= query_at, scored(query_ref, keys_ref, own), UNSEEN)
    peak = jnp.max(masked, axis=0, keepdims=True)
    weights = jnp.exp2(masked - peak)
    top[...] = peak
    bottom[...] = jnp.sum(weights, axis=0, keepdims=True)
    summed[...] = mixed_values(own_ref, other_ref, 0, own, weights)
    visit(meta_ref, 0, query_ref, keys_ref, own_ref, other_ref, top, bottom, summed)


def far_kernel(
    meta_ref,
    query_ref,
    keys_ref,
    own_ref,
    other_ref,
    near_top,
    near_bottom,
    near_summed,
    out_ref,
    top,
    bottom,
    summed,
):
    top[...] = near_top[...]
    bottom[...] = near_bottom[...]
    summed[...] = near_summed[...]
    visit(meta_ref, 1, query_ref, keys_ref, own_ref, other_ref, top, bottom, summed)
    seg_len = keys_ref.shape[3]
    scaled = summed[...] / bottom[...]
    result = jnp.zeros((1, seg_len), jnp.float32)
    for h in range(query_ref.shape[1] // seg_len):
        part = scaled[:, h * seg_len : (h + 1) * seg_len]
        result += part[h : h + 1] + part[2 + h : 3 + h]
    for i in range(out_ref.shape[0]):
        out_ref[i] = result


def finish_kernel(parts_ref, resid_ref, live_ref, last_ref, out_ref, leaf_ref):
    total = resid_ref[...] + jnp.sum(parts_ref[...], axis=0)
    values = jnp.where(live_ref[...] > 0.5, total, 0.0)
    out_ref[...] = values
    leaf = jnp.sum(jnp.where(last_ref[...] > 0.5, values, 0.0), axis=1, keepdims=True)
    leaf_ref[...] = jnp.broadcast_to(leaf, leaf_ref.shape)


def gathered(value, axis):
    return lax.all_to_all(value, axis, 0, 0)


def on_device(
    tokens, w_query, key_weight, value_weight, resid_head, head_readout, parents, placed, lengths
):
    seg_len, model_width = tokens.shape
    segments = parents.shape[0]
    fsdp_size = lax.axis_size(FSDP)
    quarters = lax.axis_size("x")
    pairs = segments // 2
    width = key_weight.shape[1]
    rows = width + 8
    heads = w_query.shape[1] // HEAD_SIZE
    swap = [(0, 1), (1, 0)]
    params = pltpu.CompilerParams(vmem_limit_bytes=VMEM_LIMIT)

    sent = jnp.broadcast_to(value_weight.T[None], (quarters, width, seg_len))
    other = lax.ppermute(w_query, "zl", swap)
    values_x = gathered(sent, "x")
    readout = head_readout.reshape(heads, HEAD_SIZE).astype(jnp.float32)
    own_readout = lax.dynamic_slice(
        resid_head, (lax.axis_index(SEG) * seg_len,), (seg_len,)
    )
    key_rows = jnp.concatenate(
        [
            jnp.pad(key_weight.T.astype(jnp.float32), ((0, 4), (0, 0))),
            jnp.pad(own_readout.astype(jnp.float32)[None], ((0, 3), (0, 0))),
        ]
    )
    both = jnp.pad(w_query, ((0, w_query.shape[0]), (0, 0)))
    values_x, readout, key_rows, both = lax.optimization_barrier(
        (values_x, readout, key_rows, both)
    )
    both = lax.dynamic_update_slice(both, other, (w_query.shape[0], 0))
    pieces = pl.pallas_call(
        weights_kernel,
        out_shape=jax.ShapeDtypeStruct((pairs, rows, seg_len), jnp.bfloat16),
        in_specs=[VMEM_SPEC] * 3,
        out_specs=VMEM_SPEC,
        compiler_params=params,
        cost_estimate=pl.CostEstimate(flops=2**33, bytes_accessed=2**12, transcendentals=0),
        name="fold_weights",
    )(values_x, readout, key_rows)
    pieces, both = lax.optimization_barrier((pieces, both))
    query_weight = lax.all_gather(both, ("y", "c"), axis=0, tiled=True)

    near_weights = gathered(pieces, ("y", "zl"))
    by_token = jax.ShapeDtypeStruct((1, seg_len), jnp.float32)
    meta, table, positions, spans = pl.pallas_call(
        tree_kernel,
        out_shape=(
            jax.ShapeDtypeStruct((META,), jnp.int32),
            jax.ShapeDtypeStruct((segments, 128), jnp.float32),
            by_token,
            by_token,
        ),
        in_specs=[HBM_SPEC] * 3,
        out_specs=(SMEM_SPEC,) + (VMEM_SPEC,) * 3,
        scratch_shapes=[pltpu.SMEM((segments,), jnp.int32)] * 4
        + [pltpu.SemaphoreType.DMA((3,))],
        compiler_params=params,
        name="tree",
    )(parents, placed, lengths)
    dims = jnp.arange(HEAD_SIZE, dtype=jnp.int32)
    frequency = ROPE_BASE ** (-2.0 * (dims // 2).astype(jnp.float32) / HEAD_SIZE)
    angles = frequency[:, None] * positions
    cosine = jnp.cos(angles)
    sine = jnp.sin(angles) * jnp.where(dims % 2 == 0, -1.0, 1.0)[:, None]
    near_weights, cosine, sine, spans = lax.optimization_barrier(
        (near_weights, cosine, sine, spans)
    )

    far_weights = lax.ppermute(near_weights, "c", swap)
    live, last = pl.pallas_call(
        masks_kernel,
        out_shape=(by_token, by_token),
        in_specs=[VMEM_SPEC],
        out_specs=(VMEM_SPEC,) * 2,
        compiler_params=params,
        cost_estimate=pl.CostEstimate(flops=2**33, bytes_accessed=2**12, transcendentals=0),
        name="masks",
    )(spans)
    near_weights, live, last = lax.optimization_barrier((near_weights, live, last))
    near_sums = pl.pallas_call(
        near_keys_kernel,
        out_shape=jax.ShapeDtypeStruct((rows, seg_len), jnp.float32),
        in_specs=[VMEM_SPEC] * 2,
        out_specs=VMEM_SPEC,
        compiler_params=params,
        cost_estimate=pl.CostEstimate(
            flops=rows * seg_len * model_width, bytes_accessed=2**21, transcendentals=0
        ),
        name="project_near_keys",
    )(tokens, near_weights)
    far_weights, near_sums = lax.optimization_barrier((far_weights, near_sums))
    keys, residual = pl.pallas_call(
        far_keys_kernel,
        out_shape=(
            jax.ShapeDtypeStruct((lax.axis_size("y"), rows, seg_len), jnp.bfloat16),
            jax.ShapeDtypeStruct((1, seg_len), jnp.float32),
        ),
        in_specs=[VMEM_SPEC] * 5,
        out_specs=(VMEM_SPEC, VMEM_SPEC),
        scratch_shapes=[pltpu.VMEM((rows, seg_len), jnp.float32)],
        compiler_params=params,
        name="project_far_keys",
    )(tokens, far_weights, near_sums, cosine, sine)

    keys_y = gathered(keys, "y")
    spread = lax.axis_size(("zl", "x"))
    values = keys_y[:, width:]
    keys_y = keys_y[:, :width]
    copies = pl.pallas_call(
        spread_kernel,
        out_shape=jax.ShapeDtypeStruct((spread, *keys_y.shape), keys_y.dtype),
        in_specs=[VMEM_SPEC],
        out_specs=HBM_SPEC,
        scratch_shapes=[pltpu.SemaphoreType.DMA((spread,))],
        compiler_params=params,
        name="spread_keys",
    )(keys_y)
    near = gathered(copies, ("zl", "x"))
    values = jnp.stack([values, lax.ppermute(values, "c", swap)])
    values, query_sine = lax.optimization_barrier((values, sine))
    other_values = lax.ppermute(values, "zl", swap)
    queries = pl.pallas_call(
        queries_kernel,
        out_shape=jax.ShapeDtypeStruct((HEAD_SIZE, heads * seg_len), jnp.bfloat16),
        in_specs=[VMEM_SPEC] * 4,
        out_specs=VMEM_SPEC,
        scratch_shapes=[pltpu.VMEM((seg_len, heads * HEAD_SIZE), jnp.float32)],
        cost_estimate=pl.CostEstimate(
            flops=2 * seg_len * model_width * heads * HEAD_SIZE,
            bytes_accessed=2 * model_width * (seg_len + heads * HEAD_SIZE),
            transcendentals=0,
        ),
        compiler_params=params,
        name="project_queries",
    )(tokens, query_weight.reshape(segments, seg_len, -1), cosine, query_sine)
    near, queries, other_values = lax.optimization_barrier((near, queries, other_values))
    far = lax.ppermute(near, "c", swap)
    columns = heads * seg_len
    state = (
        jax.ShapeDtypeStruct((1, columns), jnp.float32),
        jax.ShapeDtypeStruct((1, columns), jnp.float32),
        jax.ShapeDtypeStruct((8, columns), jnp.float32),
    )
    near_state = pl.pallas_call(
        near_kernel,
        out_shape=state,
        in_specs=[SMEM_SPEC] + [VMEM_SPEC] * 4,
        out_specs=(VMEM_SPEC,) * 3,
        compiler_params=params,
        cost_estimate=pl.CostEstimate(
            flops=2**28, bytes_accessed=2**21, transcendentals=2**19
        ),
        name="attend_near",
    )(meta, queries, near, values, other_values)
    far, near_state = lax.optimization_barrier((far, near_state))
    mixed = pl.pallas_call(
        far_kernel,
        out_shape=jax.ShapeDtypeStruct((fsdp_size, 1, seg_len), jnp.float32),
        in_specs=[SMEM_SPEC] + [VMEM_SPEC] * 7,
        out_specs=VMEM_SPEC,
        scratch_shapes=[pltpu.VMEM(part.shape, part.dtype) for part in state],
        compiler_params=params,
        name="attend_far",
    )(meta, queries, far, values, other_values, *near_state)
    parts = gathered(mixed, FSDP)
    token_values, leaf_rows = pl.pallas_call(
        finish_kernel,
        out_shape=(
            jax.ShapeDtypeStruct((1, seg_len), jnp.float32),
            jax.ShapeDtypeStruct((segments, 128), jnp.float32),
        ),
        in_specs=[VMEM_SPEC] * 4,
        out_specs=(VMEM_SPEC, VMEM_SPEC),
        compiler_params=params,
        name="token_values",
    )(parts, residual, live, last)
    leaves = gathered(leaf_rows, SEG)
    branch = jnp.sum(leaves * table, axis=0)[:segments]
    return (token_values.reshape(seg_len), branch)


def solution(mesh):
    fine = Mesh(mesh.devices.reshape(8, 2, 2, 4, 4), SEG + FSDP)
    in_specs = (
        P(SEG, None),
        P(SEG, FSDP),
        P(SEG, FSDP),
        P(SEG, FSDP),
        P(),
        P(FSDP),
        P(),
        P(),
        P(),
    )
    out_specs = (P(SEG), P())
    return jax.shard_map(
        on_device, mesh=fine, in_specs=in_specs, out_specs=out_specs, check_vma=False
    )
```

```python
import jax
import jax.numpy as jnp
from jax import lax
from jax.experimental import pallas as pl
from jax.experimental.pallas import tpu as pltpu
from jax.sharding import Mesh
from jax.sharding import PartitionSpec as P

KEY_VALUE_HEADS = 4
HEAD_SIZE = 128
ROPE_BASE = 1000000.0
SEG = ("y", "zl", "c")
FSDP = ("zh", "x")
NEAR, FAR, LENGTHS, META = 8, 48, 80, 168
UNSEEN = -1e30
LOG2_E = 1.4426950408889634
VMEM_LIMIT = 40 * 1024 * 1024

VMEM_SPEC = pl.BlockSpec(memory_space=pltpu.VMEM)
SMEM_SPEC = pl.BlockSpec(memory_space=pltpu.SMEM)
HBM_SPEC = pl.BlockSpec(memory_space=pltpu.HBM)


def tree_kernel(
    parents_src,
    placed_src,
    lengths_src,
    meta_ref,
    table_ref,
    position_ref,
    span_ref,
    parents_ref,
    placed_ref,
    lengths_ref,
    slot_of,
    sems,
):
    copies = [
        pltpu.make_async_copy(source, there, sems.at[i])
        for i, (source, there) in enumerate(
            ((parents_src, parents_ref), (placed_src, placed_ref), (lengths_src, lengths_ref))
        )
    ]
    for copy in copies:
        copy.start()
    for copy in copies:
        copy.wait()
    segments = parents_ref.shape[0]
    slot = lax.axis_index(SEG)
    own = placed_ref[slot]

    def place(j, carry):
        slot_of[placed_ref[j]] = j
        return carry

    lax.fori_loop(0, segments, place, 0)

    def clear(j, carry):
        meta_ref[j] = 0
        return carry

    lax.fori_loop(0, META, clear, 0)

    def above(state):
        seg, near, far, offset = state
        there = slot_of[seg]
        is_near = (there % 2 == slot % 2).astype(jnp.int32)
        entry = jnp.where(is_near == 1, NEAR + near, FAR + far)
        meta_ref[entry] = there
        meta_ref[LENGTHS + entry] = lengths_ref[seg]
        return parents_ref[seg], near + is_near, far + 1 - is_near, offset + lengths_ref[seg]

    zero = jnp.int32(0)
    _, near, far, offset = lax.while_loop(
        lambda state: state[0] >= 0, above, (parents_ref[own], zero, zero, zero)
    )
    meta_ref[0] = near
    meta_ref[1] = far
    index = lax.broadcasted_iota(jnp.int32, position_ref.shape, 1)
    position_ref[...] = (offset + index).astype(jnp.float32)
    span_ref[...] = (lengths_ref[own] - index).astype(jnp.float32)

    row = lax.broadcasted_iota(jnp.int32, (128, 128), 0)
    col = lax.broadcasted_iota(jnp.int32, (128, 128), 1)
    row_s = lax.broadcasted_iota(jnp.int32, (segments, 128), 0)
    col_s = lax.broadcasted_iota(jnp.int32, (segments, 128), 1)
    parent_of = jnp.full((segments, 128), -1, jnp.int32)
    held = jnp.full((segments, 128), -1, jnp.int32)
    for i in range(segments):
        parent_of = jnp.where(row_s == i, parents_ref[i], parent_of)
        held = jnp.where(row_s == i, placed_ref[i], held)
    step = jnp.where(parent_of == col_s, 1.0, 0.0)
    step = jnp.concatenate([step, jnp.zeros((128 - segments, 128), jnp.float32)], axis=0)
    ancestry = jnp.where(row == col, 1.0, 0.0) + step

    def times(a, b):
        return jnp.dot(
            a.astype(jnp.bfloat16), b.astype(jnp.bfloat16), preferred_element_type=jnp.float32
        )

    power = step
    reach = 1
    while 2 * reach <= segments:
        power = times(power, power)
        ancestry = ancestry + times(power, ancestry)
        reach *= 2
    children = jnp.sum(step, axis=0, keepdims=True)
    leafy = jnp.where((children < 0.5) & (col[:1] < segments), 1.0, 0.0)
    leaves = times(jnp.broadcast_to(leafy, (8, 128)), ancestry)[:1]
    placement = jnp.where(held == col_s, 1.0, 0.0)
    share = times(placement * leafy, ancestry)
    table_ref[...] = jnp.where(col_s < segments, share / jnp.maximum(leaves, 1.0), 0.0)


def weights_kernel(value_ref, readout_ref, key_ref, out_ref):
    quarters, part, rows = value_ref.shape
    value = value_ref[...].reshape(quarters * part, rows)
    readout = readout_ref[...].astype(jnp.bfloat16)
    folded = jnp.dot(readout, value, preferred_element_type=jnp.float32)
    high = folded.astype(jnp.bfloat16).astype(jnp.float32)
    low = folded - high
    width = key_ref.shape[0] - 8
    piece = jnp.concatenate([key_ref[:width], high, low, key_ref[width + 4 :]], axis=0)
    piece = piece.astype(jnp.bfloat16)
    for i in range(out_ref.shape[0]):
        out_ref[i] = piece


def masks_kernel(span_ref, live_ref, last_ref):
    live_ref[...] = jnp.where(span_ref[...] > 0.5, 1.0, 0.0)
    last_ref[...] = jnp.where(jnp.abs(span_ref[...] - 1.0) < 0.5, 1.0, 0.0)


def turned(raw, cosine, sine, axis):
    extent = raw.shape[axis]
    index = lax.broadcasted_iota(jnp.int32, raw.shape, axis)
    after = pltpu.roll(raw, extent - 1, axis)
    before = pltpu.roll(raw, 1, axis)
    return raw * cosine + jnp.where(index % 2 == 0, after, before) * sine


def half_projected(tokens_ref, weights_ref, total, parity):
    for even in range(2):

        @pl.when(parity == even)
        def _():
            blocks, _, depth = weights_ref.shape
            acc = total[...]
            for p in range(blocks):
                start = (2 * p + even) * depth
                acc += lax.dot_general(
                    weights_ref[p],
                    tokens_ref[:, start : start + depth],
                    (((1,), (1,)), ((), ())),
                    preferred_element_type=jnp.float32,
                )
            total[...] = acc


def near_keys_kernel(tokens_ref, weights_ref, out_ref):
    out_ref[...] = jnp.zeros_like(out_ref)
    half_projected(tokens_ref, weights_ref, out_ref, lax.axis_index("c"))


def far_keys_kernel(
    tokens_ref, weights_ref, near_ref, cosine_ref, sine_ref, out_ref, resid_ref, total
):
    total[...] = near_ref[...]
    half_projected(tokens_ref, weights_ref, total, 1 - lax.axis_index("c"))
    width = total.shape[0] - 8
    start = pl.multiple_of(lax.axis_index("x") * width, width)
    keys = turned(total[:width], cosine_ref[pl.ds(start, width)], sine_ref[pl.ds(start, width)], 0)
    last = total[width:]
    row = lax.broadcasted_iota(jnp.int32, last.shape, 0)
    summed = last + pltpu.roll(last, 6, 0)
    high = summed.astype(jnp.bfloat16).astype(jnp.float32)
    low = pltpu.roll(summed - high, 2, 0)
    tail = jnp.where(row < 2, high, jnp.where(row < 4, low, 0.0))
    resid_ref[...] = last[4:5]
    piece = jnp.concatenate([keys, tail], axis=0).astype(jnp.bfloat16)
    for i in range(out_ref.shape[0]):
        out_ref[i] = piece


def queries_kernel(tokens_ref, weights_ref, cosine_ref, sine_ref, out_ref, total):
    blocks, depth, _ = weights_ref.shape
    seg_len = tokens_ref.shape[0]
    half = lax.axis_index("zl")
    for upper in range(2):

        @pl.when(half == upper)
        def _():
            acc = jnp.zeros_like(total)
            for i in range(blocks):
                block = i // 4 * 4 + (i % 2 ^ upper) * 2 + i // 2 % 2
                acc += jnp.dot(
                    tokens_ref[:, block * depth : (block + 1) * depth],
                    weights_ref[i],
                    preferred_element_type=jnp.float32,
                )
            total[...] = acc

    raw = total[...].T
    for h in range(raw.shape[0] // HEAD_SIZE):
        head = raw[h * HEAD_SIZE : (h + 1) * HEAD_SIZE]
        out_ref[:, h * seg_len : (h + 1) * seg_len] = turned(
            head, cosine_ref[...], sine_ref[...], 0
        ).astype(jnp.bfloat16)


def spread_kernel(keys_ref, out_ref, sems):
    copies = [
        pltpu.make_async_copy(
            keys_ref.at[:, pl.ds(0, out_ref.shape[2])], out_ref.at[i], sems.at[i]
        )
        for i in range(out_ref.shape[0])
    ]
    for copy in copies:
        copy.start()
    for copy in copies:
        copy.wait()


def scored(query_ref, keys_ref, slot):
    quarters = lax.axis_size("x")
    seg_len = keys_ref.shape[3]
    keys = keys_ref[pl.ds(slot // 2 % 2 * quarters, quarters), slot // 4]
    raw = lax.dot_general(
        keys.reshape(HEAD_SIZE, seg_len),
        query_ref[...],
        (((0,), (0,)), ((), ())),
        preferred_element_type=jnp.float32,
    )
    return raw * (HEAD_SIZE ** (-0.5) * LOG2_E)


def valued(own_ref, other_ref, far, slot, weights):
    is_other = slot // 2 % 2 != lax.axis_index("zl")
    own, other = (ref[far, slot // 4].astype(jnp.float32) for ref in (own_ref, other_ref))
    rows = jnp.where(is_other, other, own)
    columns = (rows + pltpu.roll(rows, 6, 0)).T
    keys = columns.shape[0]
    heads = weights.shape[1] // keys
    return weights * jnp.concatenate(
        [jnp.broadcast_to(columns[:, h : h + 1], (keys, keys)) for h in range(heads)], axis=1
    )


def visit(meta_ref, far, query_ref, keys_ref, own_ref, other_ref, top, bottom, summed):
    key_at = lax.broadcasted_iota(jnp.int32, (keys_ref.shape[3], query_ref.shape[1]), 0)[:, :1]
    first = (NEAR, FAR)[far]

    def two(n, carry):
        entries = [first + 2 * n, first + 2 * n + 1]
        slots = [meta_ref[e] for e in entries]
        masked = [
            scored(query_ref, keys_ref, slot)
            + jnp.where(key_at < meta_ref[LENGTHS + e], 0.0, UNSEEN)
            for e, slot in zip(entries, slots)
        ]
        peak = jnp.max(jnp.maximum(masked[0], masked[1]), axis=0, keepdims=True)
        peak = jnp.maximum(top[...], peak)
        shrink = jnp.exp2(top[...] - peak)
        weights = [jnp.exp2(m - peak) for m in masked]
        top[...] = peak
        bottom[...] = bottom[...] * shrink + jnp.sum(
            weights[0] + weights[1], axis=0, keepdims=True
        )
        summed[...] = summed[...] * shrink + jnp.sum(
            valued(own_ref, other_ref, far, slots[0], weights[0])
            + valued(own_ref, other_ref, far, slots[1], weights[1]),
            axis=0,
            keepdims=True,
        )
        return carry

    lax.fori_loop(0, (meta_ref[far] + 1) // 2, two, 0)


def near_kernel(meta_ref, query_ref, keys_ref, own_ref, other_ref, top, bottom, summed):
    seg_len = keys_ref.shape[3]
    shape = (seg_len, query_ref.shape[1])
    key_at = lax.broadcasted_iota(jnp.int32, shape, 0)
    query_at = lax.broadcasted_iota(jnp.int32, shape, 1) % seg_len
    own = lax.axis_index(SEG)
    masked = jnp.where(key_at <= query_at, scored(query_ref, keys_ref, own), UNSEEN)
    peak = jnp.max(masked, axis=0, keepdims=True)
    weights = jnp.exp2(masked - peak)
    top[...] = peak
    bottom[...] = jnp.sum(weights, axis=0, keepdims=True)
    summed[...] = jnp.sum(
        valued(own_ref, other_ref, 0, own, weights), axis=0, keepdims=True
    )
    visit(meta_ref, 0, query_ref, keys_ref, own_ref, other_ref, top, bottom, summed)


def far_kernel(
    meta_ref,
    query_ref,
    keys_ref,
    own_ref,
    other_ref,
    near_top,
    near_bottom,
    near_summed,
    out_ref,
    top,
    bottom,
    summed,
):
    top[...] = near_top[...]
    bottom[...] = near_bottom[...]
    summed[...] = near_summed[...]
    visit(meta_ref, 1, query_ref, keys_ref, own_ref, other_ref, top, bottom, summed)
    seg_len = keys_ref.shape[3]
    scaled = summed[...] / bottom[...]
    result = jnp.zeros((1, seg_len), jnp.float32)
    for h in range(query_ref.shape[1] // seg_len):
        result += scaled[:, h * seg_len : (h + 1) * seg_len]
    for i in range(out_ref.shape[0]):
        out_ref[i] = result


def finish_kernel(parts_ref, resid_ref, live_ref, last_ref, out_ref, leaf_ref):
    total = resid_ref[...] + jnp.sum(parts_ref[...], axis=0)
    values = jnp.where(live_ref[...] > 0.5, total, 0.0)
    out_ref[...] = values
    leaf = jnp.sum(jnp.where(last_ref[...] > 0.5, values, 0.0), axis=1, keepdims=True)
    leaf_ref[...] = jnp.broadcast_to(leaf, leaf_ref.shape)


def gathered(value, axis):
    return lax.all_to_all(value, axis, 0, 0)


def on_device(
    tokens, w_query, key_weight, value_weight, resid_head, head_readout, parents, placed, lengths
):
    seg_len, model_width = tokens.shape
    segments = parents.shape[0]
    fsdp_size = lax.axis_size(FSDP)
    quarters = lax.axis_size("x")
    pairs = segments // 2
    width = key_weight.shape[1]
    rows = width + 8
    heads = w_query.shape[1] // HEAD_SIZE
    swap = [(0, 1), (1, 0)]
    params = pltpu.CompilerParams(vmem_limit_bytes=VMEM_LIMIT)

    sent = jnp.broadcast_to(value_weight.T[None], (quarters, width, seg_len))
    other = lax.ppermute(w_query, "zl", swap)
    values_x = gathered(sent, "x")
    readout = head_readout.reshape(heads, HEAD_SIZE).astype(jnp.float32)
    own_readout = lax.dynamic_slice(
        resid_head, (lax.axis_index(SEG) * seg_len,), (seg_len,)
    )
    key_rows = jnp.concatenate(
        [
            jnp.pad(key_weight.T.astype(jnp.float32), ((0, 4), (0, 0))),
            jnp.pad(own_readout.astype(jnp.float32)[None], ((0, 3), (0, 0))),
        ]
    )
    both = jnp.pad(w_query, ((0, w_query.shape[0]), (0, 0)))
    values_x, readout, key_rows, both = lax.optimization_barrier(
        (values_x, readout, key_rows, both)
    )
    both = lax.dynamic_update_slice(both, other, (w_query.shape[0], 0))
    pieces = pl.pallas_call(
        weights_kernel,
        out_shape=jax.ShapeDtypeStruct((pairs, rows, seg_len), jnp.bfloat16),
        in_specs=[VMEM_SPEC] * 3,
        out_specs=VMEM_SPEC,
        compiler_params=params,
        cost_estimate=pl.CostEstimate(flops=2**33, bytes_accessed=2**12, transcendentals=0),
        name="fold_weights",
    )(values_x, readout, key_rows)
    pieces, both = lax.optimization_barrier((pieces, both))
    query_weight = lax.all_gather(both, ("y", "c"), axis=0, tiled=True)

    near_weights = gathered(pieces, ("y", "zl"))
    by_token = jax.ShapeDtypeStruct((1, seg_len), jnp.float32)
    meta, table, positions, spans = pl.pallas_call(
        tree_kernel,
        out_shape=(
            jax.ShapeDtypeStruct((META,), jnp.int32),
            jax.ShapeDtypeStruct((segments, 128), jnp.float32),
            by_token,
            by_token,
        ),
        in_specs=[HBM_SPEC] * 3,
        out_specs=(SMEM_SPEC,) + (VMEM_SPEC,) * 3,
        scratch_shapes=[pltpu.SMEM((segments,), jnp.int32)] * 4
        + [pltpu.SemaphoreType.DMA((3,))],
        compiler_params=params,
        name="tree",
    )(parents, placed, lengths)
    dims = jnp.arange(HEAD_SIZE, dtype=jnp.int32)
    frequency = ROPE_BASE ** (-2.0 * (dims // 2).astype(jnp.float32) / HEAD_SIZE)
    angles = frequency[:, None] * positions
    cosine = jnp.cos(angles)
    sine = jnp.sin(angles) * jnp.where(dims % 2 == 0, -1.0, 1.0)[:, None]
    near_weights, cosine, sine, spans = lax.optimization_barrier(
        (near_weights, cosine, sine, spans)
    )

    far_weights = lax.ppermute(near_weights, "c", swap)
    live, last = pl.pallas_call(
        masks_kernel,
        out_shape=(by_token, by_token),
        in_specs=[VMEM_SPEC],
        out_specs=(VMEM_SPEC,) * 2,
        compiler_params=params,
        cost_estimate=pl.CostEstimate(flops=2**33, bytes_accessed=2**12, transcendentals=0),
        name="masks",
    )(spans)
    near_weights, live, last = lax.optimization_barrier((near_weights, live, last))
    near_sums = pl.pallas_call(
        near_keys_kernel,
        out_shape=jax.ShapeDtypeStruct((rows, seg_len), jnp.float32),
        in_specs=[VMEM_SPEC] * 2,
        out_specs=VMEM_SPEC,
        compiler_params=params,
        cost_estimate=pl.CostEstimate(
            flops=rows * seg_len * model_width, bytes_accessed=2**21, transcendentals=0
        ),
        name="project_near_keys",
    )(tokens, near_weights)
    far_weights, near_sums = lax.optimization_barrier((far_weights, near_sums))
    keys, residual = pl.pallas_call(
        far_keys_kernel,
        out_shape=(
            jax.ShapeDtypeStruct((lax.axis_size("y"), rows, seg_len), jnp.bfloat16),
            jax.ShapeDtypeStruct((1, seg_len), jnp.float32),
        ),
        in_specs=[VMEM_SPEC] * 5,
        out_specs=(VMEM_SPEC, VMEM_SPEC),
        scratch_shapes=[pltpu.VMEM((rows, seg_len), jnp.float32)],
        compiler_params=params,
        name="project_far_keys",
    )(tokens, far_weights, near_sums, cosine, sine)

    keys_y = gathered(keys, "y")
    spread = lax.axis_size(("zl", "x"))
    values = keys_y[:, width:]
    copies = pl.pallas_call(
        spread_kernel,
        out_shape=jax.ShapeDtypeStruct(
            (spread, keys_y.shape[0], width, seg_len), keys_y.dtype
        ),
        in_specs=[VMEM_SPEC],
        out_specs=HBM_SPEC,
        scratch_shapes=[pltpu.SemaphoreType.DMA((spread,))],
        compiler_params=params,
        name="spread_keys",
    )(keys_y)
    near = gathered(copies, ("zl", "x"))
    values = jnp.stack([values, lax.ppermute(values, "c", swap)])
    values, query_sine = lax.optimization_barrier((values, sine))
    other_values = lax.ppermute(values, "zl", swap)
    queries = pl.pallas_call(
        queries_kernel,
        out_shape=jax.ShapeDtypeStruct((HEAD_SIZE, heads * seg_len), jnp.bfloat16),
        in_specs=[VMEM_SPEC] * 4,
        out_specs=VMEM_SPEC,
        scratch_shapes=[pltpu.VMEM((seg_len, heads * HEAD_SIZE), jnp.float32)],
        cost_estimate=pl.CostEstimate(
            flops=2 * seg_len * model_width * heads * HEAD_SIZE,
            bytes_accessed=2 * model_width * (seg_len + heads * HEAD_SIZE),
            transcendentals=0,
        ),
        compiler_params=params,
        name="project_queries",
    )(tokens, query_weight.reshape(segments, seg_len, -1), cosine, query_sine)
    near, queries, other_values = lax.optimization_barrier((near, queries, other_values))
    far = lax.ppermute(near, "c", swap)
    columns = heads * seg_len
    state = (
        jax.ShapeDtypeStruct((1, columns), jnp.float32),
        jax.ShapeDtypeStruct((1, columns), jnp.float32),
        jax.ShapeDtypeStruct((1, columns), jnp.float32),
    )
    near_state = pl.pallas_call(
        near_kernel,
        out_shape=state,
        in_specs=[SMEM_SPEC] + [VMEM_SPEC] * 4,
        out_specs=(VMEM_SPEC,) * 3,
        compiler_params=params,
        cost_estimate=pl.CostEstimate(
            flops=2**28, bytes_accessed=2**21, transcendentals=2**19
        ),
        name="attend_near",
    )(meta, queries, near, values, other_values)
    far, near_state = lax.optimization_barrier((far, near_state))
    mixed = pl.pallas_call(
        far_kernel,
        out_shape=jax.ShapeDtypeStruct((fsdp_size, 1, seg_len), jnp.float32),
        in_specs=[SMEM_SPEC] + [VMEM_SPEC] * 7,
        out_specs=VMEM_SPEC,
        scratch_shapes=[pltpu.VMEM(part.shape, part.dtype) for part in state],
        compiler_params=params,
        name="attend_far",
    )(meta, queries, far, values, other_values, *near_state)
    parts = gathered(mixed, FSDP)
    token_values, leaf_rows = pl.pallas_call(
        finish_kernel,
        out_shape=(
            jax.ShapeDtypeStruct((1, seg_len), jnp.float32),
            jax.ShapeDtypeStruct((segments, 128), jnp.float32),
        ),
        in_specs=[VMEM_SPEC] * 4,
        out_specs=(VMEM_SPEC, VMEM_SPEC),
        compiler_params=params,
        name="token_values",
    )(parts, residual, live, last)
    leaves = gathered(leaf_rows, SEG)
    branch = jnp.sum(leaves * table, axis=0)[:segments]
    return (token_values.reshape(seg_len), branch)


def solution(mesh):
    fine = Mesh(mesh.devices.reshape(8, 2, 2, 4, 4), SEG + FSDP)
    in_specs = (
        P(SEG, None),
        P(SEG, FSDP),
        P(SEG, FSDP),
        P(SEG, FSDP),
        P(),
        P(FSDP),
        P(),
        P(),
        P(),
    )
    out_specs = (P(SEG), P())
    return jax.shard_map(
        on_device, mesh=fine, in_specs=in_specs, out_specs=out_specs, check_vma=False
    )
```
